32 devices in a mesh: dp: 2 (over y), seq: 16 (over z, x, core).
Axes of the slice: x: 2, y: 2, z: 4, core: 2. Of those that a mesh axis runs over, the one named last changes fastest.
Arguments:
- tokens: bfloat16 [2, 256, 128, 512], P('dp', None, 'seq'), may hold values from -6 to 6
- patch_mask: int32 [2, 256, 128], P('dp', None, 'seq'), may hold values 0 or 1
- mask_token: float32 [512], replicated, may hold values from -6 to 6
- gain: float32 [512], replicated, may hold values from 0.1 to 1.9
- w_qkv: bfloat16 [512, 1536], replicated, may hold values from -0.25 to 0.25
- w_out: bfloat16 [512, 512], replicated, may hold values from -0.25 to 0.25
- block_ids: int32 [256], replicated, may hold values from 0 to 3, as said below
- temporal_mask: int32 [8, 8], replicated, may hold values from 0 to 1, as said below
- cotangent: bfloat16 [2, 256, 128, 512], P('dp', None, 'seq'), may hold values from -6 to 6
Outputs:
- layer_out: bfloat16 [2, 256, 128, 512], P('dp', None, 'seq')
- qkv_grad: float32 [1536, 512], P('seq')
- out_grad: float32 [512, 512], P('seq')
The draws below stay inside these ranges and needn't reach their ends.
Inputs may be any that keep to these rules, and one draw needn't show every extreme that they name: `block_ids`: each block id is held by exactly 64 electrodes. `temporal_mask`: every diagonal entry is 1.
All inputs are finite; a program needn't handle non-finite values. No bound on the sum of `patch_mask` on one device may be relied on, other than what follows from the above.
Results may differ from the reference program's by a relative error of at most 0.0092.
Values may be sent and summed in bfloat16 or wider, within the bound.
A program may use at most 128 MiB of HBM per device.

```python
import jax
import jax.numpy as jnp
from jax import lax

E = 256
P_SIZE = 128
HEADS = 8
HEAD_DIM = 64
EB = 64
TB = 16
D = 512
RECS = 2


def draw_block_ids(key, part):
    return (jax.random.permutation(key, E) // EB).astype(jnp.int32)


def draw_temporal_mask(key, part):
    random_bits = jax.random.randint(key, (P_SIZE // TB, P_SIZE // TB), 0, 2).astype(jnp.int32)
    diagonal = jnp.eye(P_SIZE // TB, dtype=jnp.int32)
    return jnp.maximum(random_bits, diagonal).astype(jnp.int32)


def touch_ends(drawn, rng, least, largest):
    spot = [jax.random.randint(jax.random.fold_in(rng, axis), (), 0, length) for axis, length in enumerate(drawn.shape)]
    main_axis = drawn.shape.index(max(drawn.shape))
    neighbour = spot[:main_axis] + [(spot[main_axis] + 1) % drawn.shape[main_axis]] + spot[main_axis + 1:]
    return drawn.at[tuple(spot)].set(least).at[tuple(neighbour)].set(largest)


def raised(drawn, own_key, source, target, parts, factor):
    owner, partner = [(jnp.arange(drawn.shape[axis_at]) // (drawn.shape[axis_at] // parts)).reshape([-1 if axis == axis_at else 1 for axis in range(drawn.ndim)]) for axis_at in (source, target)]
    chosen = jax.random.permutation(own_key, parts)[partner]
    strong = (owner == chosen) | (owner == (partner + parts // 2) % parts)
    return jnp.where(strong, factor * drawn, drawn)


def level_of(rng, dims, cuts, low, top_value):
    def one(dim, parts):
        heights = jax.random.uniform(jax.random.fold_in(jax.random.fold_in(rng, 6), dim), (parts,), jnp.float32, low / len(cuts), top_value / len(cuts))
        return jnp.repeat(jnp.exp(heights), dims[dim] // parts).reshape((-1,) + (1,) * (len(dims) - dim - 1))

    factor_of = one(*cuts[0])
    for cut in cuts[1:]:
        factor_of = factor_of * one(*cut)
    return factor_of


def noise(key, shape, width, reach, shards=(), kind=jnp.bfloat16):
    array = width * jax.random.normal(key, shape, jnp.float32)
    if shards:
        array = array * level_of(key, shape, shards, -0.22, 0.18)
    return jnp.clip(array, -reach, reach).astype(kind)


def gaussian_with(own_key, extent, deviation, bound, pieces, heavy, kind=jnp.bfloat16):
    entries = deviation * jax.random.normal(own_key, extent, jnp.float32)
    if pieces:
        entries = entries * level_of(own_key, extent, pieces, -0.22, 0.18)
    return jnp.clip(raised(entries, jax.random.fold_in(own_key, 3), *heavy), -bound, bound).astype(kind)


def setup_inputs(seed: int = 0) -> dict:
    key_list = jax.random.split(jax.random.key(seed), 10)
    return {
        "tokens": noise(key_list[0], (RECS, E, P_SIZE, D), 1.0, 6.0, ((0, 2), (2, 16))),
        "patch_mask": touch_ends((jax.random.randint(key_list[1], (RECS, E, P_SIZE), 0, 2) < 1).astype(jnp.int32), jax.random.fold_in(key_list[1], 1), 0, 1),
        "mask_token": noise(key_list[2], (D,), 1.0, 6.0, (), jnp.float32),
        "gain": jnp.clip(1.0 + 0.18 * jax.random.normal(key_list[3], (D,), jnp.float32), 0.1, 1.9),
        "w_qkv": noise(key_list[4], (D, 3 * D), D ** -0.5, 0.25),
        "w_out": noise(key_list[5], (D, D), D ** -0.5, 0.25),
        "block_ids": draw_block_ids(jax.random.fold_in(key_list[9], 71), 0),
        "temporal_mask": draw_temporal_mask(jax.random.fold_in(key_list[9], 71), 0),
        "cotangent": gaussian_with(key_list[8], (RECS, E, P_SIZE, D), 1.0, 6.0, ((0, 2), (2, 16)), (2, 3, 16, 2.0)),
    }


NORM_EPS = 1e-05

def stored(tensor):
    return lax.optimization_barrier(tensor.astype(jnp.bfloat16))

def normed_input(tokens, patch_mask, mask_token, gain):
    masked = jnp.where(patch_mask[..., None] == 1, mask_token, tokens.astype(jnp.float32))
    row_mean = lax.optimization_barrier(jnp.mean(masked, axis=-1, keepdims=True))
    centred = masked - row_mean
    spread = lax.optimization_barrier(jnp.mean(centred * centred, axis=-1, keepdims=True))
    normed = stored(centred * lax.rsqrt(spread + NORM_EPS) * gain)
    return (masked, normed)

def forward_attend(queries, key_rows, values, allowed, factor):
    scores = jnp.einsum('anhd,amhd->ahnm', queries.astype(jnp.float32), key_rows.astype(jnp.float32)) * factor
    exponent = jnp.exp(scores) * allowed
    weights = exponent / lax.optimization_barrier(jnp.sum(exponent, axis=-1, keepdims=True))
    rounded = stored(weights)
    output = stored(jnp.einsum('ahnm,amhd->anhd', rounded.astype(jnp.float32), values.astype(jnp.float32)))
    return (output, weights, rounded)

def backward_attend(queries, key_rows, values, weights, rounded, grad_out, factor):
    grad_float = grad_out.astype(jnp.float32)
    grad_values = stored(jnp.einsum('ahnm,anhd->amhd', rounded.astype(jnp.float32), grad_float))
    grad_weights = jnp.einsum('anhd,amhd->ahnm', grad_float, values.astype(jnp.float32))
    inner_sum = lax.optimization_barrier(jnp.sum(grad_weights * weights, axis=-1, keepdims=True))
    grad_scores = stored(weights * (grad_weights - inner_sum)).astype(jnp.float32)
    grad_queries = stored(jnp.einsum('ahnm,amhd->anhd', grad_scores, key_rows.astype(jnp.float32)) * factor)
    grad_keys = stored(jnp.einsum('ahnm,anhd->amhd', grad_scores, queries.astype(jnp.float32)) * factor)
    return (grad_queries, grad_keys, grad_values)

def reference(tokens, patch_mask, mask_token, gain, w_qkv, w_out, block_ids, temporal_mask, cotangent):
    half_width = D // 2
    heads_half = HEADS // 2
    factor = HEAD_DIM ** (-0.5)
    same_block = (block_ids[:, None] == block_ids[None, :]).astype(jnp.float32)
    patch_block = (jnp.arange(P_SIZE) // TB).astype(jnp.int32)
    time_allowed = temporal_mask[patch_block][:, patch_block].astype(jnp.float32)

    def per_record(totals, inputs):
        record_tokens, record_mask, record_cot = inputs
        masked, normed = normed_input(record_tokens, record_mask, mask_token, gain)
        normed_flat = normed.reshape(E * P_SIZE, D)
        projected = stored(jnp.dot(normed_flat, w_qkv, preferred_element_type=jnp.float32))
        projected = projected.reshape(E, P_SIZE, 6, heads_half, HEAD_DIM)
        spatial = jnp.transpose(projected[:, :, :3], (1, 0, 2, 3, 4))
        space_out, space_weights, space_rounded = forward_attend(spatial[:, :, 0], spatial[:, :, 1], spatial[:, :, 2], same_block, factor)
        time_out, time_weights, time_rounded = forward_attend(projected[:, :, 3], projected[:, :, 4], projected[:, :, 5], time_allowed, factor)
        attended = jnp.concatenate([jnp.transpose(space_out, (1, 0, 2, 3)).reshape(E, P_SIZE, half_width), time_out.reshape(E, P_SIZE, half_width)], axis=-1)
        attended_flat = attended.reshape(E * P_SIZE, D)
        layer_out = (masked.reshape(E * P_SIZE, D) + jnp.dot(attended_flat, w_out, preferred_element_type=jnp.float32)).astype(jnp.bfloat16)
        cot_flat = record_cot.reshape(E * P_SIZE, D)
        out_grad = jnp.dot(cot_flat.T, attended_flat, preferred_element_type=jnp.float32)
        attended_grad = stored(jnp.dot(cot_flat, w_out.T, preferred_element_type=jnp.float32)).reshape(E, P_SIZE, D)
        space_grad = jnp.transpose(attended_grad[:, :, :half_width].reshape(E, P_SIZE, heads_half, HEAD_DIM), (1, 0, 2, 3))
        space_grads = backward_attend(spatial[:, :, 0], spatial[:, :, 1], spatial[:, :, 2], space_weights, space_rounded, space_grad, factor)
        time_grad = attended_grad[:, :, half_width:].reshape(E, P_SIZE, heads_half, HEAD_DIM)
        time_grads = backward_attend(projected[:, :, 3], projected[:, :, 4], projected[:, :, 5], time_weights, time_rounded, time_grad, factor)
        spatial_grad = jnp.transpose(jnp.stack(space_grads, axis=2), (1, 0, 2, 3, 4))
        temporal_grad = jnp.stack(time_grads, axis=2)
        projected_grad = jnp.concatenate([spatial_grad, temporal_grad], axis=2).reshape(E * P_SIZE, 3 * D)
        qkv_grad = jnp.dot(projected_grad.T, normed_flat, preferred_element_type=jnp.float32)
        return ((totals[0] + qkv_grad, totals[1] + out_grad), layer_out.reshape(E, P_SIZE, D))
    initial = (jnp.zeros((3 * D, D), jnp.float32), jnp.zeros((D, D), jnp.float32))
    totals, layer_out = lax.scan(per_record, initial, (tokens, patch_mask, cotangent))
    grad_scale = 1.0 / (RECS * E * P_SIZE) ** 0.5
    return (layer_out, totals[0] * grad_scale, totals[1] * grad_scale)
```

```python
import functools
import math

import jax
import jax.numpy as jnp
from jax import lax
from jax.experimental import pallas as pl
from jax.experimental.pallas import tpu as pltpu
from jax.sharding import PartitionSpec as P

HEADS = 8
HEAD_DIM = 64
NORM_EPS = 1e-05
LANES = 128
F32 = jnp.float32
BF16 = jnp.bfloat16
VMEM_BYTES = 48 * 1024 * 1024


def dot(a, b, ca=1, cb=0):
    return lax.dot_general(a, b, (((ca,), (cb,)), ((), ())), preferred_element_type=F32)


def params():
    return pltpu.CompilerParams(vmem_limit_bytes=VMEM_BYTES)


def full(shape):
    return pl.BlockSpec(shape, lambda i: (0,) * len(shape))


def rows_of(rows, columns):
    return pl.BlockSpec((rows, columns), lambda i: (i, 0))


def scatter_rows(scratch, value, rows=slice(None)):
    for c in range(scratch.shape[0]):
        scratch[c, rows, :] = value[:, c * LANES : (c + 1) * LANES].astype(F32)


def gather_rows(scratch, rows):
    return jnp.concatenate(
        [scratch[c, rows, :] for c in range(scratch.shape[0])], axis=1
    )


def masked_rows(tokens, mask, mask_token):
    return jnp.where(mask == 1.0, mask_token, tokens.astype(F32))


def attention_weights(q, k, allowed):
    scores = dot(q, k, 1, 1) * (HEAD_DIM**-0.5)
    exponent = jnp.where(allowed, jnp.exp(scores), 0.0)
    return exponent / jnp.sum(exponent, axis=-1, keepdims=True)


def attention_grads(q, k, v, g, weights, rounded):
    factor = HEAD_DIM**-0.5
    grad_v = dot(rounded, g, 0, 0).astype(BF16)
    grad_w = dot(g, v, 1, 1)
    inner = jnp.sum(grad_w * weights, axis=-1, keepdims=True)
    grad_s = (weights * (grad_w - inner)).astype(BF16)
    grad_q = (dot(grad_s, k) * factor).astype(BF16)
    grad_k = (dot(grad_s, q, 0, 0) * factor).astype(BF16)
    return grad_q, grad_k, grad_v


def head_columns(qkv, h, half):
    at = h * HEAD_DIM
    return [qkv[:, part * half + at : part * half + at + HEAD_DIM] for part in range(3)]


def prepare_kernel(tokens, mask, mask_token, gain, w_out, cot, send, grad_space):
    width = tokens.shape[1]
    half = width // 2
    masked = masked_rows(tokens[...], mask[...], mask_token[...])
    centred = masked - jnp.mean(masked, axis=-1, keepdims=True)
    spread = jnp.mean(centred * centred, axis=-1, keepdims=True)
    send[:, :width] = (centred * lax.rsqrt(spread + NORM_EPS) * gain[...]).astype(BF16)
    grad = dot(cot[...], w_out[...], 1, 1).astype(BF16)
    send[:, width:] = grad[:, half:]
    grad_space[...] = grad[:, :half]


def space_kernel(
    patches, normed, grad, cot, w, id_col, id_row, out, qkv_grad, out_grad,
    n_scr, g_scr, c_scr, o_scr, q_acc, o_acc,
):
    p = pl.program_id(0)
    rows = normed.shape[0]
    half = grad.shape[1]
    electrodes = id_col.shape[0]

    @pl.when(p == 0)
    def _():
        scatter_rows(n_scr, normed[...])
        scatter_rows(g_scr, grad[...])
        scatter_rows(c_scr, cot[...])
        q_acc[...] = jnp.zeros_like(q_acc)
        o_acc[...] = jnp.zeros_like(o_acc)

    mine = pl.ds(p, electrodes, stride=patches)
    n = gather_rows(n_scr, mine).astype(BF16)
    g = gather_rows(g_scr, mine).astype(BF16)
    c = gather_rows(c_scr, mine).astype(BF16)
    allowed = id_col[...] == id_row[...]
    qkv = dot(n, w[...]).astype(BF16)
    outs, grads = [], [[], [], []]
    for h in range(half // HEAD_DIM):
        q, k, v = head_columns(qkv, h, half)
        gh = g[:, h * HEAD_DIM : (h + 1) * HEAD_DIM]
        weights = attention_weights(q, k, allowed)
        rounded = weights.astype(BF16)
        outs.append(dot(rounded, v).astype(BF16))
        for part, value in zip(grads, attention_grads(q, k, v, gh, weights, rounded)):
            part.append(value)
    o = jnp.concatenate(outs, axis=1)
    scatter_rows(o_scr, o, mine)
    projected_grad = jnp.concatenate(grads[0] + grads[1] + grads[2], axis=1)
    q_acc[...] += dot(projected_grad, n, 0, 0)
    o_acc[...] += dot(c, o, 0, 0)

    @pl.when(p == patches - 1)
    def _():
        out[...] = gather_rows(o_scr, slice(None)).astype(BF16)
        qkv_grad[...] = q_acc[...].astype(BF16)
        out_grad[...] = o_acc[...].astype(BF16)


def time_forward_kernel(owned, local, direct, recv, w, allowed, out, normed, grad, qkv, scr, o_scr):
    width = normed.shape[1]
    half = grad.shape[1]
    steps = owned * local
    groups = recv.shape[0] // steps
    length = groups * local
    if direct:
        for s in range(groups):
            block = recv[s * steps : (s + 1) * steps, :].astype(F32)
            scr[:, s * local : (s + 1) * local, :] = block.reshape(owned, local, width + half)
    may = allowed[...] > 0.0

    @pl.loop(0, owned)
    def _(e):
        at = pl.ds(pl.multiple_of(e * length, length), length)
        if direct:
            block = scr[e].astype(BF16)
        else:
            block = recv[at, :]
        n = block[:, :width]
        normed[at, :] = n
        grad[at, :] = block[:, width:]
        mine = dot(n, w[...]).astype(BF16)
        qkv[at, :] = mine
        outs = []
        for h in range(half // HEAD_DIM):
            q, k, v = head_columns(mine, h, half)
            rounded = attention_weights(q, k, may).astype(BF16)
            outs.append(dot(rounded, v).astype(BF16))
        o = jnp.concatenate(outs, axis=1)
        if direct:
            o_scr[e] = o.astype(F32)
        else:
            out[at, :] = o

    if direct:
        for s in range(groups):
            block = o_scr[:, s * local : (s + 1) * local, :]
            out[s * steps : (s + 1) * steps, :] = block.reshape(steps, half).astype(BF16)


def time_backward_kernel(length, normed, grad, qkv, allowed, qkv_grad, acc):
    i = pl.program_id(0)
    half = grad.shape[1]
    may = allowed[...] > 0.0

    @pl.when(i == 0)
    def _():
        acc[...] = jnp.zeros_like(acc)

    both = []
    for e in range(normed.shape[0] // length):
        at = slice(e * length, (e + 1) * length)
        mine, g = qkv[at, :], grad[at, :]
        grads = [[], [], []]
        for h in range(half // HEAD_DIM):
            q, k, v = head_columns(mine, h, half)
            gh = g[:, h * HEAD_DIM : (h + 1) * HEAD_DIM]
            weights = attention_weights(q, k, may)
            found = attention_grads(q, k, v, gh, weights, weights.astype(BF16))
            for part, value in zip(grads, found):
                part.append(value)
        both.append(jnp.concatenate(grads[0] + grads[1] + grads[2], axis=1))
    acc[...] += dot(jnp.concatenate(both, axis=0), normed[...], 0, 0)

    @pl.when(i == pl.num_programs(0) - 1)
    def _():
        qkv_grad[...] = acc[...].astype(BF16)


def finish_kernel(tokens, mask, mask_token, space, time, w_out, cot, layer_out, out_grad, acc):
    i = pl.program_id(0)

    @pl.when(i == 0)
    def _():
        acc[...] = jnp.zeros_like(acc)

    t = time[...]
    attended = jnp.concatenate([space[...], t], axis=1)
    masked = masked_rows(tokens[...], mask[...], mask_token[...])
    layer_out[...] = (masked + dot(attended, w_out[...])).astype(BF16)
    acc[...] += dot(cot[...], t, 0, 0)

    @pl.when(i == pl.num_programs(0) - 1)
    def _():
        out_grad[...] = acc[...].astype(BF16)


def shape(rows, columns, kind=BF16):
    return jax.ShapeDtypeStruct((rows, columns), kind)


def sum_shares(terms):
    total = terms[0].astype(F32)
    for s in range(1, terms.shape[0]):
        total = total + terms[s].astype(F32)
    return total


def reduce_parts(parts, parts_out, scale):
    def exchange(value, groups):
        value = value.reshape(groups, value.shape[0] // groups, value.shape[1])
        return sum_shares(lax.all_to_all(value, "seq", split_axis=0, concat_axis=0))

    groups = lax.axis_size("seq")
    totals = [exchange(value, groups) for value in (parts, parts_out)]
    cut = totals[0].shape[0]
    total = jnp.concatenate(totals, axis=0).astype(BF16)
    copies = lax.axis_size("dp")
    if copies == 2:
        other = lax.ppermute(total, "dp", [(0, 1), (1, 0)])
        whole = total.astype(F32) + other.astype(F32)
    else:
        whole = sum_shares(lax.all_gather(total, "dp"))
    whole = whole * scale
    return whole[:cut], whole[cut:]


def shards(tokens, patch_mask, mask_token, gain, w_qkv, w_out, block_ids, temporal_mask, cotangent):
    record_count, electrodes, local, width = tokens.shape
    half = width // 2
    groups = lax.axis_size("seq")
    owned = electrodes // groups
    length = groups * local
    count = electrodes * local
    tile = min(256, count)
    steps = count // tile
    tokens_flat = tokens.reshape(count, width)
    cot = cotangent.reshape(count, width)
    mask = patch_mask.reshape(count, 1).astype(F32)
    mask_token = mask_token.reshape(1, width)
    gain = gain.reshape(1, width)
    ids = block_ids.astype(F32)
    blocks = temporal_mask.shape[0]
    onehot = (
        jnp.arange(length)[:, None] // (length // blocks) == jnp.arange(blocks)[None, :]
    ).astype(F32)
    allowed = jnp.dot(jnp.dot(onehot, temporal_mask.astype(F32)), onehot.T)

    send, grad_space = pl.pallas_call(
        prepare_kernel,
        grid=(steps,),
        in_specs=[
            rows_of(tile, width), rows_of(tile, 1), full((1, width)), full((1, width)),
            full((width, width)), rows_of(tile, width),
        ],
        out_specs=[rows_of(tile, width + half), rows_of(tile, half)],
        out_shape=[shape(count, width + half), shape(count, half)],
        compiler_params=params(),
        cost_estimate=pl.CostEstimate(
            flops=2 * count * width * width, bytes_accessed=9 * count * width, transcendentals=0
        ),
    )(tokens_flat, mask, mask_token, gain, w_out, cot)

    direct = local % 8 == 0
    recv = lax.all_to_all(
        send.reshape(groups, owned, local, width + half), "seq", split_axis=0, concat_axis=0
    )
    if not direct:
        recv = jnp.swapaxes(recv, 0, 1)
    recv = recv.reshape(count, width + half)

    space_out, grad_qkv_space, grad_out_space = pl.pallas_call(
        functools.partial(space_kernel, local),
        grid=(local,),
        in_specs=[
            full((count, width)), full((count, half)), full((count, width)),
            full((width, 3 * half)), full((electrodes, 1)), full((1, electrodes)),
        ],
        out_specs=[full((count, half)), full((3 * half, width)), full((width, half))],
        out_shape=[shape(count, half), shape(3 * half, width), shape(width, half)],
        scratch_shapes=[
            pltpu.VMEM((width // LANES, count, LANES), F32),
            pltpu.VMEM((half // LANES, count, LANES), F32),
            pltpu.VMEM((width // LANES, count, LANES), F32),
            pltpu.VMEM((half // LANES, count, LANES), F32),
            pltpu.VMEM((3 * half, width), F32),
            pltpu.VMEM((width, half), F32),
        ],
        compiler_params=params(),
        cost_estimate=pl.CostEstimate(
            flops=32 * count * width * width, bytes_accessed=8 * count * width, transcendentals=0
        ),
    )(send, grad_space, cot, w_qkv, ids.reshape(electrodes, 1), ids.reshape(1, electrodes))

    time_out, normed_time, grad_time, qkv_time = pl.pallas_call(
        functools.partial(time_forward_kernel, owned, local, direct),
        grid=(1,),
        in_specs=[
            full((count, width + half)),
            pl.BlockSpec((width, 3 * half), lambda i: (0, 1)),
            full((length, length)),
        ],
        out_specs=[
            full((count, half)), full((count, width)), full((count, half)), full((count, 3 * half)),
        ],
        out_shape=[
            shape(count, half), shape(count, width), shape(count, half), shape(count, 3 * half),
        ],
        scratch_shapes=[
            pltpu.VMEM((owned, length, width + half), F32),
            pltpu.VMEM((owned, length, half), F32),
        ],
        compiler_params=params(),
        cost_estimate=pl.CostEstimate(
            flops=6 * count * width * width, bytes_accessed=8 * count * width, transcendentals=0
        ),
    )(recv, w_qkv, allowed)

    if direct:
        back = time_out.reshape(groups, owned, local, half)
    else:
        back = jnp.swapaxes(time_out.reshape(owned, groups, local, half), 0, 1)
    time_back = lax.all_to_all(back, "seq", split_axis=0, concat_axis=0).reshape(count, half)

    pair = 2 * length if owned % 2 == 0 else length
    grad_qkv_time = pl.pallas_call(
        functools.partial(time_backward_kernel, length),
        grid=(count // pair,),
        in_specs=[
            rows_of(pair, width), rows_of(pair, half), rows_of(pair, 3 * half),
            full((length, length)),
        ],
        out_specs=full((3 * half, width)),
        out_shape=shape(3 * half, width),
        scratch_shapes=[pltpu.VMEM((3 * half, width), F32)],
        compiler_params=params(),
        cost_estimate=pl.CostEstimate(
            flops=16 * count * width * width, bytes_accessed=8 * count * width, transcendentals=0
        ),
    )(normed_time, grad_time, qkv_time, allowed)

    layer_out, grad_out_time = pl.pallas_call(
        finish_kernel,
        grid=(steps,),
        in_specs=[
            rows_of(tile, width), rows_of(tile, 1), full((1, width)), rows_of(tile, half),
            rows_of(tile, half), full((width, width)), rows_of(tile, width),
        ],
        out_specs=[rows_of(tile, width), full((width, half))],
        out_shape=[shape(count, width), shape(width, half)],
        scratch_shapes=[pltpu.VMEM((width, half), F32)],
        compiler_params=params(),
        cost_estimate=pl.CostEstimate(
            flops=4 * count * width * width, bytes_accessed=8 * count * width, transcendentals=0
        ),
    )(tokens_flat, mask, mask_token, space_out, time_back, w_out, cot)

    grad_qkv = jnp.concatenate([grad_qkv_space, grad_qkv_time], axis=0)
    grad_out = jnp.concatenate([grad_out_space, grad_out_time], axis=1)
    scale = 1.0 / math.sqrt(record_count * lax.axis_size("dp") * electrodes * length)
    share_qkv, share_out = reduce_parts(grad_qkv, grad_out, scale)
    return layer_out.reshape(tokens.shape), share_qkv, share_out


def solution(mesh):
    return jax.shard_map(
        shards,
        mesh=mesh,
        in_specs=(
            P("dp", None, "seq", None),
            P("dp", None, "seq"),
            P(),
            P(),
            P(),
            P(),
            P(),
            P(),
            P("dp", None, "seq", None),
        ),
        out_specs=(P("dp", None, "seq", None), P("seq", None), P("seq", None)),
        check_vma=False,
    )
```

```python
import functools
import math

import jax
import jax.numpy as jnp
from jax import lax
from jax.experimental import pallas as pl
from jax.experimental.pallas import tpu as pltpu
from jax.sharding import PartitionSpec as P

HEADS = 8
HEAD_DIM = 64
NORM_EPS = 1e-05
LANES = 128
F32 = jnp.float32
BF16 = jnp.bfloat16
VMEM_BYTES = 48 * 1024 * 1024


def dot(a, b, ca=1, cb=0):
    return lax.dot_general(a, b, (((ca,), (cb,)), ((), ())), preferred_element_type=F32)


def params():
    return pltpu.CompilerParams(vmem_limit_bytes=VMEM_BYTES)


def full(shape):
    return pl.BlockSpec(shape, lambda i: (0,) * len(shape))


def rows_of(rows, columns):
    return pl.BlockSpec((rows, columns), lambda i: (i, 0))


def scatter_rows(scratch, value, rows=slice(None)):
    for c in range(scratch.shape[0]):
        scratch[c, rows, :] = value[:, c * LANES : (c + 1) * LANES].astype(F32)


def gather_rows(scratch, rows):
    return jnp.concatenate(
        [scratch[c, rows, :] for c in range(scratch.shape[0])], axis=1
    )


def masked_rows(tokens, mask, mask_token):
    return jnp.where(mask == 1.0, mask_token, tokens.astype(F32))


def attention_weights(q, k, allowed):
    exponent = jnp.where(allowed, jnp.exp(dot(q, k, 1, 1)), 0.0)
    return exponent * (1.0 / jnp.sum(exponent, axis=-1, keepdims=True))


def attention_grads(q, k, v, g, weights, rounded):
    grad_v = dot(rounded, g, 0, 0).astype(BF16)
    grad_w = dot(g, v, 1, 1)
    inner = jnp.sum(grad_w * weights, axis=-1, keepdims=True)
    grad_s = (weights * (grad_w - inner)).astype(BF16)
    grad_q = (dot(grad_s, k) * (HEAD_DIM**-0.5)).astype(BF16)
    grad_k = dot(grad_s, q, 0, 0).astype(BF16)
    return grad_q, grad_k, grad_v


def head_columns(qkv, h, half):
    at = h * HEAD_DIM
    q, k, v = [qkv[:, part * half + at : part * half + at + HEAD_DIM] for part in range(3)]
    return (q.astype(F32) * (HEAD_DIM**-0.5)).astype(BF16), k, v


def prepare_kernel(
    share, tokens, mask, mask_token, gain, w_out, cot, normed, grad_space, first, second
):
    width = tokens.shape[1]
    half = width // 2
    masked = masked_rows(tokens[...], mask[...], mask_token[...])
    centred = masked - jnp.mean(masked, axis=-1, keepdims=True)
    spread = jnp.mean(centred * centred, axis=-1, keepdims=True)
    n = (centred * lax.rsqrt(spread + NORM_EPS) * gain[...]).astype(BF16)
    normed[...] = n
    grad = dot(cot[...], w_out[...], 1, 1).astype(BF16)
    grad_space[...] = grad[:, :half]
    for s in range(tokens.shape[0] // share // 2):
        for which, send in enumerate((first, second)):
            to = slice(s * share, (s + 1) * share)
            at = slice((2 * s + which) * share, (2 * s + which + 1) * share)
            send[to, :width] = n[at, :]
            send[to, width:] = grad[at, half:]


def space_kernel(
    patches, normed, grad, cot, w, id_col, id_row, out, qkv_grad, out_grad,
    n_scr, g_scr, c_scr, o_scr, q_acc, o_acc,
):
    p = pl.program_id(0)
    rows = normed.shape[0]
    half = grad.shape[1]
    electrodes = id_col.shape[0]

    @pl.when(p == 0)
    def _():
        scatter_rows(n_scr, normed[...])
        scatter_rows(g_scr, grad[...])
        scatter_rows(c_scr, cot[...])
        q_acc[...] = jnp.zeros_like(q_acc)
        o_acc[...] = jnp.zeros_like(o_acc)

    mine = pl.ds(p, electrodes, stride=patches)
    n = gather_rows(n_scr, mine).astype(BF16)
    g = gather_rows(g_scr, mine).astype(BF16)
    c = gather_rows(c_scr, mine).astype(BF16)
    allowed = id_col[...] == id_row[...]
    qkv = dot(n, w[...]).astype(BF16)
    outs, grads = [], [[], [], []]
    for h in range(half // HEAD_DIM):
        q, k, v = head_columns(qkv, h, half)
        gh = g[:, h * HEAD_DIM : (h + 1) * HEAD_DIM]
        weights = attention_weights(q, k, allowed)
        rounded = weights.astype(BF16)
        outs.append(dot(rounded, v).astype(BF16))
        for part, value in zip(grads, attention_grads(q, k, v, gh, weights, rounded)):
            part.append(value)
    o = jnp.concatenate(outs, axis=1)
    scatter_rows(o_scr, o, mine)
    projected_grad = jnp.concatenate(grads[0] + grads[1] + grads[2], axis=1)
    q_acc[...] += dot(projected_grad, n, 0, 0)
    o_acc[...] += dot(c, o, 0, 0)

    @pl.when(p == patches - 1)
    def _():
        out[...] = gather_rows(o_scr, slice(None)).astype(BF16)
        qkv_grad[...] = q_acc[...].astype(BF16)
        out_grad[...] = o_acc[...].astype(BF16)


def time_forward_kernel(owned, local, direct, recv, w, allowed, out, normed, grad, qkv, scr, o_scr):
    width = normed.shape[1]
    half = grad.shape[1]
    steps = owned * local
    groups = recv.shape[0] // steps
    length = groups * local
    if direct:
        for s in range(groups):
            block = recv[s * steps : (s + 1) * steps, :].astype(F32)
            scr[:, s * local : (s + 1) * local, :] = block.reshape(owned, local, width + half)
    may = allowed[...] > 0.0

    def one(e):
        at = pl.ds(pl.multiple_of(e * length, length), length)
        if direct:
            block = scr[e].astype(BF16)
        else:
            block = recv[at, :]
        n = block[:, :width]
        normed[at, :] = n
        grad[at, :] = block[:, width:]
        mine = dot(n, w[...]).astype(BF16)
        qkv[at, :] = mine
        outs = []
        for h in range(half // HEAD_DIM):
            q, k, v = head_columns(mine, h, half)
            rounded = attention_weights(q, k, may).astype(BF16)
            outs.append(dot(rounded, v).astype(BF16))
        o = jnp.concatenate(outs, axis=1)
        if direct:
            o_scr[e] = o.astype(F32)
        else:
            out[at, :] = o

    together = 2 if owned % 2 == 0 else 1

    @pl.loop(0, owned // together)
    def _(i):
        for e in range(together):
            one(i * together + e)

    if direct:
        for s in range(groups):
            block = o_scr[:, s * local : (s + 1) * local, :]
            out[s * steps : (s + 1) * steps, :] = block.reshape(steps, half).astype(BF16)


def time_backward_kernel(length, normed, grad, qkv, allowed, qkv_grad, acc):
    i = pl.program_id(0)
    half = grad.shape[1]
    may = allowed[...] > 0.0

    @pl.when(i == 0)
    def _():
        acc[...] = jnp.zeros_like(acc)

    both = []
    for e in range(normed.shape[0] // length):
        at = slice(e * length, (e + 1) * length)
        mine, g = qkv[at, :], grad[at, :]
        grads = [[], [], []]
        for h in range(half // HEAD_DIM):
            q, k, v = head_columns(mine, h, half)
            gh = g[:, h * HEAD_DIM : (h + 1) * HEAD_DIM]
            weights = attention_weights(q, k, may)
            found = attention_grads(q, k, v, gh, weights, weights.astype(BF16))
            for part, value in zip(grads, found):
                part.append(value)
        both.append(jnp.concatenate(grads[0] + grads[1] + grads[2], axis=1))
    acc[...] += dot(jnp.concatenate(both, axis=0), normed[...], 0, 0)

    @pl.when(i == pl.num_programs(0) - 1)
    def _():
        qkv_grad[...] = acc[...].astype(BF16)


def finish_kernel(tokens, mask, mask_token, space, time, w_out, cot, layer_out, out_grad, acc):
    i = pl.program_id(0)

    @pl.when(i == 0)
    def _():
        acc[...] = jnp.zeros_like(acc)

    t = time[...]
    attended = jnp.concatenate([space[...], t], axis=1)
    masked = masked_rows(tokens[...], mask[...], mask_token[...])
    layer_out[...] = (masked + dot(attended, w_out[...])).astype(BF16)
    acc[...] += dot(cot[...], t, 0, 0)

    @pl.when(i == pl.num_programs(0) - 1)
    def _():
        out_grad[...] = acc[...].astype(BF16)


def shape(rows, columns, kind=BF16):
    return jax.ShapeDtypeStruct((rows, columns), kind)


def sum_shares(terms):
    total = terms[0].astype(F32)
    for s in range(1, terms.shape[0]):
        total = total + terms[s].astype(F32)
    return total


def reduce_part(value, scale):
    groups = lax.axis_size("seq")
    pairs = groups // 2
    value = value.reshape(pairs, 2, value.shape[0] // groups, value.shape[1])
    odd = lax.axis_index("seq") % 2 == 1
    sent = jnp.where(odd, value[:, 0], value[:, 1])
    kept = jnp.where(odd, value[:, 1], value[:, 0])
    got = lax.ppermute(sent, "seq", [(i, i ^ 1) for i in range(groups)])
    both = (kept.astype(F32) + got.astype(F32)).astype(BF16)
    sides = [list(range(side, groups, 2)) for side in range(2)]
    terms = lax.all_to_all(both, "seq", split_axis=0, concat_axis=0, axis_index_groups=sides)
    total = sum_shares(terms).astype(BF16)
    if lax.axis_size("dp") == 2:
        other = lax.ppermute(total, "dp", [(0, 1), (1, 0)])
        whole = total.astype(F32) + other.astype(F32)
    else:
        whole = sum_shares(lax.all_gather(total, "dp"))
    return total, whole * scale


def shards(tokens, patch_mask, mask_token, gain, w_qkv, w_out, block_ids, temporal_mask, cotangent):
    record_count, electrodes, local, width = tokens.shape
    half = width // 2
    groups = lax.axis_size("seq")
    owned = electrodes // groups
    length = groups * local
    count = electrodes * local
    tile = min(256, count)
    steps = count // tile
    tokens_flat = tokens.reshape(count, width)
    cot = cotangent.reshape(count, width)
    mask = patch_mask.reshape(count, 1).astype(F32)
    mask_token = mask_token.reshape(1, width)
    gain = gain.reshape(1, width)
    ids = block_ids.astype(F32)
    blocks = temporal_mask.shape[0]
    onehot = (
        jnp.arange(length)[:, None] // (length // blocks) == jnp.arange(blocks)[None, :]
    ).astype(F32)
    allowed = jnp.dot(jnp.dot(onehot, temporal_mask.astype(F32)), onehot.T)

    owned_half = owned // 2
    share = owned_half * local
    some = count // 2
    normed, grad_space, send_first, send_second = pl.pallas_call(
        functools.partial(prepare_kernel, share),
        grid=(steps,),
        in_specs=[
            rows_of(tile, width), rows_of(tile, 1), full((1, width)), full((1, width)),
            full((width, width)), rows_of(tile, width),
        ],
        out_specs=[
            rows_of(tile, width), rows_of(tile, half),
            rows_of(tile // 2, width + half), rows_of(tile // 2, width + half),
        ],
        out_shape=[
            shape(count, width), shape(count, half),
            shape(some, width + half), shape(some, width + half),
        ],
        compiler_params=params(),
        cost_estimate=pl.CostEstimate(
            flops=2 * count * width * width, bytes_accessed=9 * count * width, transcendentals=0
        ),
    )(tokens_flat, mask, mask_token, gain, w_out, cot)

    direct = local % 8 == 0

    def to_electrodes(send):
        recv = lax.all_to_all(
            send.reshape(groups, owned_half, local, width + half), "seq",
            split_axis=0, concat_axis=0,
        )
        if not direct:
            recv = jnp.swapaxes(recv, 0, 1)
        return recv.reshape(some, width + half)

    recv_first = to_electrodes(send_first)

    space_out, grad_qkv_space, grad_out_space = pl.pallas_call(
        functools.partial(space_kernel, local),
        grid=(local,),
        in_specs=[
            full((count, width)), full((count, half)), full((count, width)),
            full((width, 3 * half)), full((electrodes, 1)), full((1, electrodes)),
        ],
        out_specs=[full((count, half)), full((3 * half, width)), full((width, half))],
        out_shape=[shape(count, half), shape(3 * half, width), shape(width, half)],
        scratch_shapes=[
            pltpu.VMEM((width // LANES, count, LANES), F32),
            pltpu.VMEM((half // LANES, count, LANES), F32),
            pltpu.VMEM((width // LANES, count, LANES), F32),
            pltpu.VMEM((half // LANES, count, LANES), F32),
            pltpu.VMEM((3 * half, width), F32),
            pltpu.VMEM((width, half), F32),
        ],
        compiler_params=params(),
        cost_estimate=pl.CostEstimate(
            flops=32 * count * width * width, bytes_accessed=8 * count * width, transcendentals=0
        ),
    )(normed, grad_space, cot, w_qkv, ids.reshape(electrodes, 1), ids.reshape(1, electrodes))

    recv_first, send_second, space_out = lax.optimization_barrier(
        (recv_first, send_second, space_out)
    )
    recv_second = to_electrodes(send_second)

    def time_forward(recv):
        return pl.pallas_call(
            functools.partial(time_forward_kernel, owned_half, local, direct),
            grid=(1,),
            in_specs=[
                full((some, width + half)),
                pl.BlockSpec((width, 3 * half), lambda i: (0, 1)),
                full((length, length)),
            ],
            out_specs=[
                full((some, half)), full((some, width)), full((some, half)),
                full((some, 3 * half)),
            ],
            out_shape=[
                shape(some, half), shape(some, width), shape(some, half), shape(some, 3 * half),
            ],
            scratch_shapes=[
                pltpu.VMEM((owned_half, length, width + half), F32),
                pltpu.VMEM((owned_half, length, half), F32),
            ],
            compiler_params=params(),
            cost_estimate=pl.CostEstimate(
                flops=16 * some * width * width, bytes_accessed=8 * some * width,
                transcendentals=0,
            ),
        )(recv, w_qkv, allowed)

    pair = 2 * length if owned_half % 2 == 0 else length

    def time_backward(normed_time, grad_time, qkv_time):
        return pl.pallas_call(
            functools.partial(time_backward_kernel, length),
            grid=(some // pair,),
            in_specs=[
                rows_of(pair, width), rows_of(pair, half), rows_of(pair, 3 * half),
                full((length, length)),
            ],
            out_specs=full((3 * half, width)),
            out_shape=shape(3 * half, width),
            scratch_shapes=[pltpu.VMEM((3 * half, width), F32)],
            compiler_params=params(),
            cost_estimate=pl.CostEstimate(
                flops=24 * some * width * width, bytes_accessed=8 * some * width,
                transcendentals=0,
            ),
        )(normed_time, grad_time, qkv_time, allowed)

    time_first, *kept_first = time_forward(recv_first)
    grad_qkv_first = time_backward(*kept_first)
    recv_second, time_first, grad_qkv_first = lax.optimization_barrier(
        (recv_second, time_first, grad_qkv_first)
    )
    time_second, *kept_second = time_forward(recv_second)

    def by_group(out):
        if direct:
            return out.reshape(groups, share, half)
        back = jnp.swapaxes(out.reshape(owned_half, groups, local, half), 0, 1)
        return back.reshape(groups, share, half)

    back = jnp.concatenate([by_group(time_first), by_group(time_second)], axis=1)
    time_back = lax.all_to_all(back, "seq", split_axis=0, concat_axis=0).reshape(count, half)
    grad_qkv_second = time_backward(*kept_second)
    grad_qkv_time = (grad_qkv_first.astype(F32) + grad_qkv_second.astype(F32)).astype(BF16)
    grad_qkv = jnp.concatenate([grad_qkv_space, grad_qkv_time], axis=0)
    time_back, grad_qkv = lax.optimization_barrier((time_back, grad_qkv))
    scale = 1.0 / math.sqrt(record_count * lax.axis_size("dp") * electrodes * length)
    total_qkv, share_qkv = reduce_part(grad_qkv, scale)

    layer_out, grad_out_time = pl.pallas_call(
        finish_kernel,
        grid=(steps,),
        in_specs=[
            rows_of(tile, width), rows_of(tile, 1), full((1, width)), rows_of(tile, half),
            rows_of(tile, half), full((width, width)), rows_of(tile, width),
        ],
        out_specs=[rows_of(tile, width), full((width, half))],
        out_shape=[shape(count, width), shape(width, half)],
        scratch_shapes=[pltpu.VMEM((width, half), F32)],
        compiler_params=params(),
        cost_estimate=pl.CostEstimate(
            flops=4 * count * width * width, bytes_accessed=8 * count * width, transcendentals=0
        ),
    )(tokens_flat, mask, mask_token, space_out, time_back, w_out, cot)

    grad_out = jnp.concatenate([grad_out_space, grad_out_time], axis=1)
    total_qkv, grad_out = lax.optimization_barrier((total_qkv, grad_out))
    _, share_out = reduce_part(grad_out, scale)
    return layer_out.reshape(tokens.shape), share_qkv, share_out


def solution(mesh):
    return jax.shard_map(
        shards,
        mesh=mesh,
        in_specs=(
            P("dp", None, "seq", None),
            P("dp", None, "seq"),
            P(),
            P(),
            P(),
            P(),
            P(),
            P(),
            P("dp", None, "seq", None),
        ),
        out_specs=(P("dp", None, "seq", None), P("seq", None), P("seq", None)),
        check_vma=False,
    )
```

```python
import functools
import math

import jax
import jax.numpy as jnp
from jax import lax
from jax.experimental import pallas as pl
from jax.experimental.pallas import tpu as pltpu
from jax.sharding import PartitionSpec as P

HEADS = 8
HEAD_DIM = 64
NORM_EPS = 1e-05
LANES = 128
F32 = jnp.float32
BF16 = jnp.bfloat16
VMEM_BYTES = 48 * 1024 * 1024


def dot(a, b, ca=1, cb=0):
    return lax.dot_general(a, b, (((ca,), (cb,)), ((), ())), preferred_element_type=F32)


def params():
    return pltpu.CompilerParams(vmem_limit_bytes=VMEM_BYTES)


def full(shape):
    return pl.BlockSpec(shape, lambda i: (0,) * len(shape))


def rows_of(rows, columns):
    return pl.BlockSpec((rows, columns), lambda i: (i, 0))


def columns_of(rows, columns):
    return pl.BlockSpec((rows, columns), lambda i: (0, i))


def scatter_rows(scratch, value, rows=slice(None)):
    for c in range(scratch.shape[0]):
        scratch[c, rows, :] = value[:, c * LANES : (c + 1) * LANES].astype(F32)


def gather_rows(scratch, rows):
    return jnp.concatenate(
        [scratch[c, rows, :] for c in range(scratch.shape[0])], axis=1
    )


def masked_rows(tokens, mask, mask_token):
    return jnp.where(mask == 1.0, mask_token, tokens.astype(F32))


def attention_weights(q, k, allowed):
    exponent = jnp.where(allowed, jnp.exp(dot(k, q, 0, 0)), 0.0)
    return exponent * (1.0 / jnp.sum(exponent, axis=0, keepdims=True))


def attention_grads(q, k, v, g, weights, rounded):
    grad_v = dot(g, rounded, 1, 1).astype(BF16)
    grad_w = dot(v, g, 0, 0)
    inner = jnp.sum(grad_w * weights, axis=0, keepdims=True)
    grad_s = (weights * (grad_w - inner)).astype(BF16)
    grad_q = (dot(k, grad_s) * (HEAD_DIM**-0.5)).astype(BF16)
    grad_k = dot(q, grad_s, 1, 1).astype(BF16)
    return grad_q, grad_k, grad_v


def head_rows(qkv, h, half):
    at = h * HEAD_DIM
    q, k, v = [qkv[part * half + at : part * half + at + HEAD_DIM, :] for part in range(3)]
    return (q.astype(F32) * (HEAD_DIM**-0.5)).astype(BF16), k, v


def transposed(value):
    return value.astype(F32).T.astype(BF16)


def prepare_kernel(
    share, tokens, mask, mask_token, gain, w_out, cot, normed, grad_space, first, second
):
    width = tokens.shape[1]
    half = width // 2
    masked = masked_rows(tokens[...], mask[...], mask_token[...])
    centred = masked - jnp.mean(masked, axis=-1, keepdims=True)
    spread = jnp.mean(centred * centred, axis=-1, keepdims=True)
    n = (centred * lax.rsqrt(spread + NORM_EPS) * gain[...]).astype(BF16)
    normed[...] = n
    grad = dot(cot[...], w_out[...], 1, 1).astype(BF16)
    grad_space[...] = grad[:, :half]
    for s in range(tokens.shape[0] // share // 2):
        for which, send in enumerate((first, second)):
            to = slice(s * share, (s + 1) * share)
            at = slice((2 * s + which) * share, (2 * s + which + 1) * share)
            send[to, :width] = n[at, :]
            send[to, width:] = grad[at, half:]


def space_kernel(
    patches, normed, grad, cot, w, id_col, id_row, out, qkv_grad, out_grad,
    n_scr, g_scr, c_scr, o_scr, q_acc, o_acc,
):
    p = pl.program_id(0)
    rows = normed.shape[0]
    half = grad.shape[1]
    electrodes = id_col.shape[0]

    @pl.when(p == 0)
    def _():
        scatter_rows(n_scr, normed[...])
        scatter_rows(g_scr, grad[...])
        scatter_rows(c_scr, cot[...])
        q_acc[...] = jnp.zeros_like(q_acc)
        o_acc[...] = jnp.zeros_like(o_acc)

    mine = pl.ds(p, electrodes, stride=patches)
    n = gather_rows(n_scr, mine).astype(BF16)
    g = gather_rows(g_scr, mine).T.astype(BF16)
    c = gather_rows(c_scr, mine).astype(BF16)
    allowed = id_col[...] == id_row[...]
    qkv = dot(w[...], n, 1, 1).astype(BF16)
    outs, grads = [], [[], [], []]
    for h in range(half // HEAD_DIM):
        q, k, v = head_rows(qkv, h, half)
        gh = g[h * HEAD_DIM : (h + 1) * HEAD_DIM, :]
        weights = attention_weights(q, k, allowed)
        rounded = weights.astype(BF16)
        outs.append(dot(v, rounded).astype(BF16))
        for part, value in zip(grads, attention_grads(q, k, v, gh, weights, rounded)):
            part.append(value)
    o = jnp.concatenate(outs, axis=0)
    scatter_rows(o_scr, o.astype(F32).T, mine)
    projected_grad = jnp.concatenate(grads[0] + grads[1] + grads[2], axis=0)
    q_acc[...] += dot(projected_grad, n)
    o_acc[...] += dot(o, c)

    @pl.when(p == patches - 1)
    def _():
        out[...] = gather_rows(o_scr, slice(None)).astype(BF16)
        qkv_grad[...] = q_acc[...].astype(BF16)
        out_grad[...] = o_acc[...].T.astype(BF16)


def time_forward_kernel(owned, local, direct, recv, w, allowed, out, normed, grad, qkv, scr, o_scr):
    width = normed.shape[1]
    half = grad.shape[0]
    steps = owned * local
    groups = recv.shape[0] // steps
    length = groups * local
    if direct:
        for s in range(groups):
            block = recv[s * steps : (s + 1) * steps, :].astype(F32)
            scr[:, s * local : (s + 1) * local, :] = block.reshape(owned, local, width + half)
    may = allowed[...] > 0.0

    def one(e):
        at = pl.ds(pl.multiple_of(e * length, length), length)
        if direct:
            block = scr[e].astype(BF16)
        else:
            block = recv[at, :]
        n = block[:, :width]
        normed[at, :] = n
        grad[:, at] = transposed(block[:, width:])
        mine = dot(w[...], n, 1, 1).astype(BF16)
        qkv[:, at] = mine
        outs = []
        for h in range(half // HEAD_DIM):
            q, k, v = head_rows(mine, h, half)
            rounded = attention_weights(q, k, may).astype(BF16)
            outs.append(dot(v, rounded).astype(BF16))
        o = jnp.concatenate(outs, axis=0).astype(F32).T
        if direct:
            o_scr[e] = o
        else:
            out[at, :] = o.astype(BF16)

    together = 2 if owned % 2 == 0 else 1

    @pl.loop(0, owned // together)
    def _(i):
        for e in range(together):
            one(i * together + e)

    if direct:
        for s in range(groups):
            block = o_scr[:, s * local : (s + 1) * local, :]
            out[s * steps : (s + 1) * steps, :] = block.reshape(steps, half).astype(BF16)


def time_backward_kernel(length, normed, grad, qkv, allowed, qkv_grad, acc):
    i = pl.program_id(0)
    half = grad.shape[0]
    may = allowed[...] > 0.0

    @pl.when(i == 0)
    def _():
        acc[...] = jnp.zeros_like(acc)

    both = []
    for e in range(normed.shape[0] // length):
        at = slice(e * length, (e + 1) * length)
        mine, g = qkv[:, at], grad[:, at]
        grads = [[], [], []]
        for h in range(half // HEAD_DIM):
            q, k, v = head_rows(mine, h, half)
            gh = g[h * HEAD_DIM : (h + 1) * HEAD_DIM, :]
            weights = attention_weights(q, k, may)
            found = attention_grads(q, k, v, gh, weights, weights.astype(BF16))
            for part, value in zip(grads, found):
                part.append(value)
        both.append(jnp.concatenate(grads[0] + grads[1] + grads[2], axis=0))
    acc[...] += dot(jnp.concatenate(both, axis=1), normed[...])

    @pl.when(i == pl.num_programs(0) - 1)
    def _():
        qkv_grad[...] = acc[...].astype(BF16)


def finish_kernel(tokens, mask, mask_token, space, time, w_out, cot, layer_out, out_grad, acc):
    i = pl.program_id(0)

    @pl.when(i == 0)
    def _():
        acc[...] = jnp.zeros_like(acc)

    t = time[...]
    attended = jnp.concatenate([space[...], t], axis=1)
    masked = masked_rows(tokens[...], mask[...], mask_token[...])
    layer_out[...] = (masked + dot(attended, w_out[...])).astype(BF16)
    acc[...] += dot(cot[...], t, 0, 0)

    @pl.when(i == pl.num_programs(0) - 1)
    def _():
        out_grad[...] = acc[...].astype(BF16)


def shape(rows, columns, kind=BF16):
    return jax.ShapeDtypeStruct((rows, columns), kind)


def sum_shares(terms):
    total = terms[0].astype(F32)
    for s in range(1, terms.shape[0]):
        total = total + terms[s].astype(F32)
    return total


def sum_pair(value):
    groups = lax.axis_size("seq")
    pairs = groups // 2
    value = value.reshape(pairs, 2, value.shape[0] // groups, value.shape[1])
    odd = lax.axis_index("seq") % 2 == 1
    sent = jnp.where(odd, value[:, 0], value[:, 1])
    kept = jnp.where(odd, value[:, 1], value[:, 0])
    got = lax.ppermute(sent, "seq", [(i, i ^ 1) for i in range(groups)])
    return (kept.astype(F32) + got.astype(F32)).astype(BF16)


def reduce_pairs(both, scale):
    groups = lax.axis_size("seq")
    sides = [list(range(side, groups, 2)) for side in range(2)]
    terms = lax.all_to_all(both, "seq", split_axis=0, concat_axis=0, axis_index_groups=sides)
    total = sum_shares(terms).astype(BF16)
    if lax.axis_size("dp") == 2:
        other = lax.ppermute(total, "dp", [(0, 1), (1, 0)])
        whole = total.astype(F32) + other.astype(F32)
    else:
        whole = sum_shares(lax.all_gather(total, "dp"))
    return total, whole * scale


def shards(tokens, patch_mask, mask_token, gain, w_qkv, w_out, block_ids, temporal_mask, cotangent):
    record_count, electrodes, local, width = tokens.shape
    half = width // 2
    groups = lax.axis_size("seq")
    owned = electrodes // groups
    length = groups * local
    count = electrodes * local
    tile = min(256, count)
    steps = count // tile
    tokens_flat = tokens.reshape(count, width)
    cot = cotangent.reshape(count, width)
    mask = patch_mask.reshape(count, 1).astype(F32)
    mask_token = mask_token.reshape(1, width)
    gain = gain.reshape(1, width)
    ids = block_ids.astype(F32)
    blocks = temporal_mask.shape[0]
    onehot = (
        jnp.arange(length)[:, None] // (length // blocks) == jnp.arange(blocks)[None, :]
    ).astype(F32)
    allowed = jnp.dot(jnp.dot(onehot, temporal_mask.astype(F32)), onehot.T).T
    w_rows = w_qkv.T

    owned_half = owned // 2
    share = owned_half * local
    some = count // 2
    normed, grad_space, send_first, send_second = pl.pallas_call(
        functools.partial(prepare_kernel, share),
        grid=(steps,),
        in_specs=[
            rows_of(tile, width), rows_of(tile, 1), full((1, width)), full((1, width)),
            full((width, width)), rows_of(tile, width),
        ],
        out_specs=[
            rows_of(tile, width), rows_of(tile, half),
            rows_of(tile // 2, width + half), rows_of(tile // 2, width + half),
        ],
        out_shape=[
            shape(count, width), shape(count, half),
            shape(some, width + half), shape(some, width + half),
        ],
        compiler_params=params(),
        cost_estimate=pl.CostEstimate(
            flops=2 * count * width * width, bytes_accessed=9 * count * width, transcendentals=0
        ),
    )(tokens_flat, mask, mask_token, gain, w_out, cot)

    direct = local % 8 == 0

    def to_electrodes(send):
        recv = lax.all_to_all(
            send.reshape(groups, owned_half, local, width + half), "seq",
            split_axis=0, concat_axis=0,
        )
        if not direct:
            recv = jnp.swapaxes(recv, 0, 1)
        return recv.reshape(some, width + half)

    recv_first = to_electrodes(send_first)

    space_out, grad_qkv_space, grad_out_space = pl.pallas_call(
        functools.partial(space_kernel, local),
        grid=(local,),
        in_specs=[
            full((count, width)), full((count, half)), full((count, width)),
            full((3 * half, width)), full((electrodes, 1)), full((1, electrodes)),
        ],
        out_specs=[full((count, half)), full((3 * half, width)), full((width, half))],
        out_shape=[shape(count, half), shape(3 * half, width), shape(width, half)],
        scratch_shapes=[
            pltpu.VMEM((width // LANES, count, LANES), F32),
            pltpu.VMEM((half // LANES, count, LANES), F32),
            pltpu.VMEM((width // LANES, count, LANES), F32),
            pltpu.VMEM((half // LANES, count, LANES), F32),
            pltpu.VMEM((3 * half, width), F32),
            pltpu.VMEM((half, width), F32),
        ],
        compiler_params=params(),
        cost_estimate=pl.CostEstimate(
            flops=32 * count * width * width, bytes_accessed=8 * count * width, transcendentals=0
        ),
    )(normed, grad_space, cot, w_rows, ids.reshape(electrodes, 1), ids.reshape(1, electrodes))

    recv_first, send_second, space_out = lax.optimization_barrier(
        (recv_first, send_second, space_out)
    )
    recv_second = to_electrodes(send_second)

    def time_forward(recv):
        return pl.pallas_call(
            functools.partial(time_forward_kernel, owned_half, local, direct),
            grid=(1,),
            in_specs=[
                full((some, width + half)),
                pl.BlockSpec((3 * half, width), lambda i: (1, 0)),
                full((length, length)),
            ],
            out_specs=[
                full((some, half)), full((some, width)), full((half, some)),
                full((3 * half, some)),
            ],
            out_shape=[
                shape(some, half), shape(some, width), shape(half, some), shape(3 * half, some),
            ],
            scratch_shapes=[
                pltpu.VMEM((owned_half, length, width + half), F32),
                pltpu.VMEM((owned_half, length, half), F32),
            ],
            compiler_params=params(),
            cost_estimate=pl.CostEstimate(
                flops=16 * some * width * width, bytes_accessed=8 * some * width,
                transcendentals=0,
            ),
        )(recv, w_rows, allowed)

    pair = 2 * length if owned_half % 2 == 0 else length

    def time_backward(normed_time, grad_time, qkv_time):
        return pl.pallas_call(
            functools.partial(time_backward_kernel, length),
            grid=(some // pair,),
            in_specs=[
                rows_of(pair, width), columns_of(half, pair), columns_of(3 * half, pair),
                full((length, length)),
            ],
            out_specs=full((3 * half, width)),
            out_shape=shape(3 * half, width),
            scratch_shapes=[pltpu.VMEM((3 * half, width), F32)],
            compiler_params=params(),
            cost_estimate=pl.CostEstimate(
                flops=24 * some * width * width, bytes_accessed=8 * some * width,
                transcendentals=0,
            ),
        )(normed_time, grad_time, qkv_time, allowed)

    time_first, *kept_first = time_forward(recv_first)
    grad_qkv_first = time_backward(*kept_first)
    recv_second, time_first, grad_qkv_first = lax.optimization_barrier(
        (recv_second, time_first, grad_qkv_first)
    )
    time_second, *kept_second = time_forward(recv_second)

    def by_group(out):
        if direct:
            return out.reshape(groups, share, half)
        back = jnp.swapaxes(out.reshape(owned_half, groups, local, half), 0, 1)
        return back.reshape(groups, share, half)

    back = jnp.concatenate([by_group(time_first), by_group(time_second)], axis=1)
    time_back = lax.all_to_all(back, "seq", split_axis=0, concat_axis=0).reshape(count, half)
    grad_qkv_second = time_backward(*kept_second)
    grad_qkv_time = (grad_qkv_first.astype(F32) + grad_qkv_second.astype(F32)).astype(BF16)
    grad_qkv = jnp.concatenate([grad_qkv_space, grad_qkv_time], axis=0)
    time_back, pair_qkv = lax.optimization_barrier((time_back, sum_pair(grad_qkv)))
    scale = 1.0 / math.sqrt(record_count * lax.axis_size("dp") * electrodes * length)
    total_qkv, share_qkv = reduce_pairs(pair_qkv, scale)

    layer_out, grad_out_time = pl.pallas_call(
        finish_kernel,
        grid=(steps,),
        in_specs=[
            rows_of(tile, width), rows_of(tile, 1), full((1, width)), rows_of(tile, half),
            rows_of(tile, half), full((width, width)), rows_of(tile, width),
        ],
        out_specs=[rows_of(tile, width), full((width, half))],
        out_shape=[shape(count, width), shape(width, half)],
        scratch_shapes=[pltpu.VMEM((width, half), F32)],
        compiler_params=params(),
        cost_estimate=pl.CostEstimate(
            flops=4 * count * width * width, bytes_accessed=8 * count * width, transcendentals=0
        ),
    )(tokens_flat, mask, mask_token, space_out, time_back, w_out, cot)

    grad_out = jnp.concatenate([grad_out_space, grad_out_time], axis=1)
    total_qkv, pair_out = lax.optimization_barrier((total_qkv, sum_pair(grad_out)))
    _, share_out = reduce_pairs(pair_out, scale)
    return layer_out.reshape(tokens.shape), share_qkv, share_out


def solution(mesh):
    return jax.shard_map(
        shards,
        mesh=mesh,
        in_specs=(
            P("dp", None, "seq", None),
            P("dp", None, "seq"),
            P(),
            P(),
            P(),
            P(),
            P(),
            P(),
            P("dp", None, "seq", None),
        ),
        out_specs=(P("dp", None, "seq", None), P("seq", None), P("seq", None)),
        check_vma=False,
    )
```

```python
import functools
import math

import jax
import jax.numpy as jnp
from jax import lax
from jax.experimental import pallas as pl
from jax.experimental.pallas import tpu as pltpu
from jax.sharding import PartitionSpec as P

HEADS = 8
HEAD_DIM = 64
NORM_EPS = 1e-05
LANES = 128
F32 = jnp.float32
BF16 = jnp.bfloat16
VMEM_BYTES = 48 * 1024 * 1024


def dot(a, b, ca=1, cb=0):
    return lax.dot_general(a, b, (((ca,), (cb,)), ((), ())), preferred_element_type=F32)


def params():
    return pltpu.CompilerParams(vmem_limit_bytes=VMEM_BYTES)


def full(shape):
    return pl.BlockSpec(shape, lambda i: (0,) * len(shape))


def rows_of(rows, columns):
    return pl.BlockSpec((rows, columns), lambda i: (i, 0))


def columns_of(rows, columns):
    return pl.BlockSpec((rows, columns), lambda i: (0, i))


def scatter_rows(scratch, value, rows=slice(None)):
    for c in range(scratch.shape[0]):
        scratch[c, rows, :] = value[:, c * LANES : (c + 1) * LANES].astype(F32)


def gather_rows(scratch, rows):
    return jnp.concatenate(
        [scratch[c, rows, :] for c in range(scratch.shape[0])], axis=1
    )


def masked_rows(tokens, mask, mask_token):
    return jnp.where(mask == 1.0, mask_token, tokens.astype(F32))


def attention_weights(q, k, allowed):
    exponent = jnp.where(allowed, jnp.exp(dot(k, q, 0, 0)), 0.0)
    return exponent * (1.0 / jnp.sum(exponent, axis=0, keepdims=True))


def attention_grads(q, k, v, g, weights, rounded):
    grad_v = dot(g, rounded, 1, 1).astype(BF16)
    grad_w = dot(v, g, 0, 0)
    inner = jnp.sum(grad_w * weights, axis=0, keepdims=True)
    grad_s = (weights * (grad_w - inner)).astype(BF16)
    grad_q = (dot(k, grad_s) * (HEAD_DIM**-0.5)).astype(BF16)
    grad_k = dot(q, grad_s, 1, 1).astype(BF16)
    return grad_q, grad_k, grad_v


def head_rows(qkv, h, half):
    at = h * HEAD_DIM
    q, k, v = [qkv[part * half + at : part * half + at + HEAD_DIM, :] for part in range(3)]
    return (q.astype(F32) * (HEAD_DIM**-0.5)).astype(BF16), k, v


def transposed(value):
    return value.astype(F32).T.astype(BF16)


def prepare_kernel(
    share, tokens, mask, mask_token, gain, w_out, cot, normed, grad_space, first, second
):
    width = tokens.shape[1]
    half = width // 2
    masked = masked_rows(tokens[...], mask[...], mask_token[...])
    centred = masked - jnp.mean(masked, axis=-1, keepdims=True)
    spread = jnp.mean(centred * centred, axis=-1, keepdims=True)
    n = (centred * lax.rsqrt(spread + NORM_EPS) * gain[...]).astype(BF16)
    normed[...] = n
    grad = dot(cot[...], w_out[...], 1, 1).astype(BF16)
    grad_space[...] = grad[:, :half]
    both = sum(share)
    for s in range(tokens.shape[0] // both):
        start = s * both
        for size, send in zip(share, (first, second)):
            to = slice(s * size, (s + 1) * size)
            at = slice(start, start + size)
            send[to, :width] = n[at, :]
            send[to, width:] = grad[at, half:]
            start += size


def space_kernel(
    patches, normed, grad, cot, w, id_col, id_row, out, qkv_grad, out_grad,
    n_scr, g_scr, c_scr, o_scr, q_acc, o_acc,
):
    p = pl.program_id(0)
    rows = normed.shape[0]
    half = grad.shape[1]
    electrodes = id_col.shape[0]

    @pl.when(p == 0)
    def _():
        scatter_rows(n_scr, normed[...])
        scatter_rows(g_scr, grad[...])
        scatter_rows(c_scr, cot[...])
        q_acc[...] = jnp.zeros_like(q_acc)
        o_acc[...] = jnp.zeros_like(o_acc)

    mine = pl.ds(p, electrodes, stride=patches)
    n = gather_rows(n_scr, mine).astype(BF16)
    g = gather_rows(g_scr, mine).T.astype(BF16)
    c = gather_rows(c_scr, mine).astype(BF16)
    allowed = id_col[...] == id_row[...]
    qkv = dot(w[...], n, 1, 1).astype(BF16)
    outs, grads = [], [[], [], []]
    for h in range(half // HEAD_DIM):
        q, k, v = head_rows(qkv, h, half)
        gh = g[h * HEAD_DIM : (h + 1) * HEAD_DIM, :]
        weights = attention_weights(q, k, allowed)
        rounded = weights.astype(BF16)
        outs.append(dot(v, rounded).astype(BF16))
        for part, value in zip(grads, attention_grads(q, k, v, gh, weights, rounded)):
            part.append(value)
    o = jnp.concatenate(outs, axis=0)
    scatter_rows(o_scr, o.astype(F32).T, mine)
    projected_grad = jnp.concatenate(grads[0] + grads[1] + grads[2], axis=0)
    q_acc[...] += dot(projected_grad, n)
    o_acc[...] += dot(o, c)

    @pl.when(p == patches - 1)
    def _():
        out[...] = gather_rows(o_scr, slice(None)).astype(BF16)
        qkv_grad[...] = q_acc[...].astype(BF16)
        out_grad[...] = o_acc[...].T.astype(BF16)


def time_forward_kernel(owned, local, direct, recv, w, allowed, out, normed, grad, qkv, scr, o_scr):
    width = normed.shape[1]
    half = grad.shape[0]
    steps = owned * local
    groups = recv.shape[0] // steps
    length = groups * local
    if direct:
        for s in range(groups):
            block = recv[s * steps : (s + 1) * steps, :].astype(F32)
            scr[:, s * local : (s + 1) * local, :] = block.reshape(owned, local, width + half)
    may = allowed[...] > 0.0

    def one(e):
        at = pl.ds(pl.multiple_of(e * length, length), length)
        if direct:
            block = scr[e].astype(BF16)
        else:
            block = recv[at, :]
        n = block[:, :width]
        normed[at, :] = n
        grad[:, at] = transposed(block[:, width:])
        mine = dot(w[...], n, 1, 1).astype(BF16)
        qkv[:, at] = mine
        outs = []
        for h in range(half // HEAD_DIM):
            q, k, v = head_rows(mine, h, half)
            rounded = attention_weights(q, k, may).astype(BF16)
            outs.append(dot(v, rounded).astype(BF16))
        o = jnp.concatenate(outs, axis=0).astype(F32).T
        if direct:
            o_scr[e] = o
        else:
            out[at, :] = o.astype(BF16)

    together = 2 if owned % 2 == 0 else 1

    @pl.loop(0, owned // together)
    def _(i):
        for e in range(together):
            one(i * together + e)

    if direct:
        for s in range(groups):
            block = o_scr[:, s * local : (s + 1) * local, :]
            out[s * steps : (s + 1) * steps, :] = block.reshape(steps, half).astype(BF16)


def time_backward_kernel(length, normed, grad, qkv, allowed, qkv_grad, acc):
    i = pl.program_id(0)
    half = grad.shape[0]
    may = allowed[...] > 0.0

    @pl.when(i == 0)
    def _():
        acc[...] = jnp.zeros_like(acc)

    both = []
    for e in range(normed.shape[0] // length):
        at = slice(e * length, (e + 1) * length)
        mine, g = qkv[:, at], grad[:, at]
        grads = [[], [], []]
        for h in range(half // HEAD_DIM):
            q, k, v = head_rows(mine, h, half)
            gh = g[h * HEAD_DIM : (h + 1) * HEAD_DIM, :]
            weights = attention_weights(q, k, may)
            found = attention_grads(q, k, v, gh, weights, weights.astype(BF16))
            for part, value in zip(grads, found):
                part.append(value)
        both.append(jnp.concatenate(grads[0] + grads[1] + grads[2], axis=0))
    acc[...] += dot(jnp.concatenate(both, axis=1), normed[...])

    @pl.when(i == pl.num_programs(0) - 1)
    def _():
        qkv_grad[...] = acc[...].astype(BF16)


def finish_kernel(tokens, mask, mask_token, space, time, w_out, cot, layer_out, out_grad, acc):
    i = pl.program_id(0)

    @pl.when(i == 0)
    def _():
        acc[...] = jnp.zeros_like(acc)

    t = time[...]
    attended = jnp.concatenate([space[...], t], axis=1)
    masked = masked_rows(tokens[...], mask[...], mask_token[...])
    layer_out[...] = (masked + dot(attended, w_out[...])).astype(BF16)
    acc[...] += dot(cot[...], t, 0, 0)

    @pl.when(i == pl.num_programs(0) - 1)
    def _():
        out_grad[...] = acc[...].astype(BF16)


def shape(rows, columns, kind=BF16):
    return jax.ShapeDtypeStruct((rows, columns), kind)


def sum_shares(terms):
    total = terms[0].astype(F32)
    for s in range(1, terms.shape[0]):
        total = total + terms[s].astype(F32)
    return total


def sum_pair(value):
    groups = lax.axis_size("seq")
    pairs = groups // 2
    value = value.reshape(pairs, 2, value.shape[0] // groups, value.shape[1])
    odd = lax.axis_index("seq") % 2 == 1
    sent = jnp.where(odd, value[:, 0], value[:, 1])
    kept = jnp.where(odd, value[:, 1], value[:, 0])
    got = lax.ppermute(sent, "seq", [(i, i ^ 1) for i in range(groups)])
    return (kept.astype(F32) + got.astype(F32)).astype(BF16)


def reduce_pairs(both, scale):
    groups = lax.axis_size("seq")
    sides = [list(range(side, groups, 2)) for side in range(2)]
    terms = lax.all_to_all(both, "seq", split_axis=0, concat_axis=0, axis_index_groups=sides)
    total = sum_shares(terms).astype(BF16)
    if lax.axis_size("dp") == 2:
        other = lax.ppermute(total, "dp", [(0, 1), (1, 0)])
        whole = total.astype(F32) + other.astype(F32)
    else:
        whole = sum_shares(lax.all_gather(total, "dp"))
    return total, whole * scale


def shards(tokens, patch_mask, mask_token, gain, w_qkv, w_out, block_ids, temporal_mask, cotangent):
    record_count, electrodes, local, width = tokens.shape
    half = width // 2
    groups = lax.axis_size("seq")
    owned = electrodes // groups
    length = groups * local
    count = electrodes * local
    tile = min(256, count)
    steps = count // tile
    tokens_flat = tokens.reshape(count, width)
    cot = cotangent.reshape(count, width)
    mask = patch_mask.reshape(count, 1).astype(F32)
    mask_token = mask_token.reshape(1, width)
    gain = gain.reshape(1, width)
    ids = block_ids.astype(F32)
    blocks = temporal_mask.shape[0]
    onehot = (
        jnp.arange(length)[:, None] // (length // blocks) == jnp.arange(blocks)[None, :]
    ).astype(F32)
    allowed = jnp.dot(jnp.dot(onehot, temporal_mask.astype(F32)), onehot.T).T
    w_rows = w_qkv.T

    step = max(1, 16 // local)
    owned_first = owned * 5 // 8 // step * step
    portions = (owned_first, owned - owned_first)
    share = tuple(portion * local for portion in portions)
    normed, grad_space, send_first, send_second = pl.pallas_call(
        functools.partial(prepare_kernel, share),
        grid=(steps,),
        in_specs=[
            rows_of(tile, width), rows_of(tile, 1), full((1, width)), full((1, width)),
            full((width, width)), rows_of(tile, width),
        ],
        out_specs=[
            rows_of(tile, width), rows_of(tile, half),
            rows_of(tile // (owned * local) * share[0], width + half),
            rows_of(tile // (owned * local) * share[1], width + half),
        ],
        out_shape=[
            shape(count, width), shape(count, half),
            shape(groups * share[0], width + half), shape(groups * share[1], width + half),
        ],
        compiler_params=params(),
        cost_estimate=pl.CostEstimate(
            flops=2 * count * width * width, bytes_accessed=9 * count * width, transcendentals=0
        ),
    )(tokens_flat, mask, mask_token, gain, w_out, cot)

    direct = local % 8 == 0

    def to_electrodes(send, portion):
        recv = lax.all_to_all(
            send.reshape(groups, portion, local, width + half), "seq",
            split_axis=0, concat_axis=0,
        )
        if not direct:
            recv = jnp.swapaxes(recv, 0, 1)
        return recv.reshape(portion * length, width + half)

    recv_first = to_electrodes(send_first, portions[0])

    space_out, grad_qkv_space, grad_out_space = pl.pallas_call(
        functools.partial(space_kernel, local),
        grid=(local,),
        in_specs=[
            full((count, width)), full((count, half)), full((count, width)),
            full((3 * half, width)), full((electrodes, 1)), full((1, electrodes)),
        ],
        out_specs=[full((count, half)), full((3 * half, width)), full((width, half))],
        out_shape=[shape(count, half), shape(3 * half, width), shape(width, half)],
        scratch_shapes=[
            pltpu.VMEM((width // LANES, count, LANES), F32),
            pltpu.VMEM((half // LANES, count, LANES), F32),
            pltpu.VMEM((width // LANES, count, LANES), F32),
            pltpu.VMEM((half // LANES, count, LANES), F32),
            pltpu.VMEM((3 * half, width), F32),
            pltpu.VMEM((half, width), F32),
        ],
        compiler_params=params(),
        cost_estimate=pl.CostEstimate(
            flops=32 * count * width * width, bytes_accessed=8 * count * width, transcendentals=0
        ),
    )(normed, grad_space, cot, w_rows, ids.reshape(electrodes, 1), ids.reshape(1, electrodes))

    recv_first, send_second, space_out = lax.optimization_barrier(
        (recv_first, send_second, space_out)
    )
    recv_second = to_electrodes(send_second, portions[1])

    def time_forward(recv, portion):
        some = portion * length
        return pl.pallas_call(
            functools.partial(time_forward_kernel, portion, local, direct),
            grid=(1,),
            in_specs=[
                full((some, width + half)),
                pl.BlockSpec((3 * half, width), lambda i: (1, 0)),
                full((length, length)),
            ],
            out_specs=[
                full((some, half)), full((some, width)), full((half, some)),
                full((3 * half, some)),
            ],
            out_shape=[
                shape(some, half), shape(some, width), shape(half, some), shape(3 * half, some),
            ],
            scratch_shapes=[
                pltpu.VMEM((portion, length, width + half), F32),
                pltpu.VMEM((portion, length, half), F32),
            ],
            compiler_params=params(),
            cost_estimate=pl.CostEstimate(
                flops=16 * some * width * width, bytes_accessed=8 * some * width,
                transcendentals=0,
            ),
        )(recv, w_rows, allowed)

    def time_backward(normed_time, grad_time, qkv_time):
        some = normed_time.shape[0]
        pair = 2 * length if some % (2 * length) == 0 else length
        return pl.pallas_call(
            functools.partial(time_backward_kernel, length),
            grid=(some // pair,),
            in_specs=[
                rows_of(pair, width), columns_of(half, pair), columns_of(3 * half, pair),
                full((length, length)),
            ],
            out_specs=full((3 * half, width)),
            out_shape=shape(3 * half, width),
            scratch_shapes=[pltpu.VMEM((3 * half, width), F32)],
            compiler_params=params(),
            cost_estimate=pl.CostEstimate(
                flops=24 * some * width * width, bytes_accessed=8 * some * width,
                transcendentals=0,
            ),
        )(normed_time, grad_time, qkv_time, allowed)

    time_first, *kept_first = time_forward(recv_first, portions[0])
    recv_second, time_first = lax.optimization_barrier((recv_second, time_first))
    time_second, *kept_second = time_forward(recv_second, portions[1])
    time_second, kept_first = lax.optimization_barrier((time_second, kept_first))
    grad_qkv_first = time_backward(*kept_first)

    def by_group(out, portion):
        if not direct:
            out = jnp.swapaxes(out.reshape(portion, groups, local, half), 0, 1)
        return out.reshape(groups, portion * local, half)

    back = jnp.concatenate(
        [by_group(time_first, portions[0]), by_group(time_second, portions[1])], axis=1
    )
    time_back = lax.all_to_all(back, "seq", split_axis=0, concat_axis=0).reshape(count, half)
    grad_qkv_second = time_backward(*kept_second)
    grad_qkv_time = (grad_qkv_first.astype(F32) + grad_qkv_second.astype(F32)).astype(BF16)
    grad_qkv = jnp.concatenate([grad_qkv_space, grad_qkv_time], axis=0)
    time_back, pair_qkv = lax.optimization_barrier((time_back, sum_pair(grad_qkv)))
    scale = 1.0 / math.sqrt(record_count * lax.axis_size("dp") * electrodes * length)
    total_qkv, share_qkv = reduce_pairs(pair_qkv, scale)

    layer_out, grad_out_time = pl.pallas_call(
        finish_kernel,
        grid=(steps,),
        in_specs=[
            rows_of(tile, width), rows_of(tile, 1), full((1, width)), rows_of(tile, half),
            rows_of(tile, half), full((width, width)), rows_of(tile, width),
        ],
        out_specs=[rows_of(tile, width), full((width, half))],
        out_shape=[shape(count, width), shape(width, half)],
        scratch_shapes=[pltpu.VMEM((width, half), F32)],
        compiler_params=params(),
        cost_estimate=pl.CostEstimate(
            flops=4 * count * width * width, bytes_accessed=8 * count * width, transcendentals=0
        ),
    )(tokens_flat, mask, mask_token, space_out, time_back, w_out, cot)

    grad_out = jnp.concatenate([grad_out_space, grad_out_time], axis=1)
    total_qkv, pair_out = lax.optimization_barrier((total_qkv, sum_pair(grad_out)))
    _, share_out = reduce_pairs(pair_out, scale)
    return layer_out.reshape(tokens.shape), share_qkv, share_out


def solution(mesh):
    return jax.shard_map(
        shards,
        mesh=mesh,
        in_specs=(
            P("dp", None, "seq", None),
            P("dp", None, "seq"),
            P(),
            P(),
            P(),
            P(),
            P(),
            P(),
            P("dp", None, "seq", None),
        ),
        out_specs=(P("dp", None, "seq", None), P("seq", None), P("seq", None)),
        check_vma=False,
    )
```

```python
import functools
import math

import jax
import jax.numpy as jnp
from jax import lax
from jax.experimental import pallas as pl
from jax.experimental.pallas import tpu as pltpu
from jax.sharding import PartitionSpec as P

HEADS = 8
HEAD_DIM = 64
NORM_EPS = 1e-05
LANES = 128
F32 = jnp.float32
BF16 = jnp.bfloat16
VMEM_BYTES = 48 * 1024 * 1024


def dot(a, b, ca=1, cb=0):
    return lax.dot_general(a, b, (((ca,), (cb,)), ((), ())), preferred_element_type=F32)


def params():
    return pltpu.CompilerParams(vmem_limit_bytes=VMEM_BYTES)


def full(shape):
    return pl.BlockSpec(shape, lambda i: (0,) * len(shape))


def rows_of(rows, columns):
    return pl.BlockSpec((rows, columns), lambda i: (i, 0))


def columns_of(rows, columns):
    return pl.BlockSpec((rows, columns), lambda i: (0, i))


def scatter_rows(scratch, value, rows=slice(None)):
    for c in range(scratch.shape[0]):
        scratch[c, rows, :] = value[:, c * LANES : (c + 1) * LANES].astype(F32)


def gather_rows(scratch, rows):
    return jnp.concatenate(
        [scratch[c, rows, :] for c in range(scratch.shape[0])], axis=1
    )


def masked_rows(tokens, mask, mask_token):
    return jnp.where(mask == 1.0, mask_token, tokens.astype(F32))


def attention_weights(q, k, allowed):
    exponent = jnp.where(allowed, jnp.exp(dot(k, q, 0, 0)), 0.0)
    return exponent * (1.0 / jnp.sum(exponent, axis=0, keepdims=True))


def attention_grads(q, k, v, g, weights, rounded):
    grad_v = dot(g, rounded, 1, 1).astype(BF16)
    grad_w = dot(v, g, 0, 0)
    inner = jnp.sum(grad_w * weights, axis=0, keepdims=True)
    grad_s = (weights * (grad_w - inner)).astype(BF16)
    grad_q = (dot(k, grad_s) * (HEAD_DIM**-0.5)).astype(BF16)
    grad_k = dot(q, grad_s, 1, 1).astype(BF16)
    return grad_q, grad_k, grad_v


def head_rows(qkv, h, half):
    at = h * HEAD_DIM
    q, k, v = [qkv[part * half + at : part * half + at + HEAD_DIM, :] for part in range(3)]
    return (q.astype(F32) * (HEAD_DIM**-0.5)).astype(BF16), k, v


def prepare_kernel(
    share, tokens, mask, mask_token, gain, w_out, cot, normed, grad_space, first, second
):
    width = tokens.shape[1]
    half = width // 2
    masked = masked_rows(tokens[...], mask[...], mask_token[...])
    centred = masked - jnp.mean(masked, axis=-1, keepdims=True)
    spread = jnp.mean(centred * centred, axis=-1, keepdims=True)
    n = (centred * lax.rsqrt(spread + NORM_EPS) * gain[...]).astype(BF16)
    normed[...] = n
    grad = dot(cot[...], w_out[...], 1, 1).astype(BF16)
    grad_space[...] = grad[:, :half]
    both = sum(share)
    for s in range(tokens.shape[0] // both):
        start = s * both
        for size, send in zip(share, (first, second)):
            to = slice(s * size, (s + 1) * size)
            at = slice(start, start + size)
            send[to, :width] = n[at, :]
            send[to, width:] = grad[at, half:]
            start += size


def space_kernel(
    patches, normed, grad, cot, w, id_col, id_row, out, qkv_grad, out_grad,
    n_scr, g_scr, c_scr, o_scr, q_acc, o_acc,
):
    p = pl.program_id(0)
    rows = normed.shape[0]
    half = grad.shape[1]
    electrodes = id_col.shape[0]

    @pl.when(p == 0)
    def _():
        scatter_rows(n_scr, normed[...])
        scatter_rows(g_scr, grad[...])
        scatter_rows(c_scr, cot[...])
        q_acc[...] = jnp.zeros_like(q_acc)
        o_acc[...] = jnp.zeros_like(o_acc)

    mine = pl.ds(p, electrodes, stride=patches)
    n = gather_rows(n_scr, mine).astype(BF16)
    g = gather_rows(g_scr, mine).T.astype(BF16)
    c = gather_rows(c_scr, mine).astype(BF16)
    allowed = id_col[...] == id_row[...]
    qkv = dot(w[...], n, 1, 1).astype(BF16)
    outs, grads = [], [[], [], []]
    for h in range(half // HEAD_DIM):
        q, k, v = head_rows(qkv, h, half)
        gh = g[h * HEAD_DIM : (h + 1) * HEAD_DIM, :]
        weights = attention_weights(q, k, allowed)
        rounded = weights.astype(BF16)
        outs.append(dot(v, rounded).astype(BF16))
        for part, value in zip(grads, attention_grads(q, k, v, gh, weights, rounded)):
            part.append(value)
    o = jnp.concatenate(outs, axis=0)
    scatter_rows(o_scr, o.astype(F32).T, mine)
    projected_grad = jnp.concatenate(grads[0] + grads[1] + grads[2], axis=0)
    q_acc[...] += dot(projected_grad, n)
    o_acc[...] += dot(o, c)

    @pl.when(p == patches - 1)
    def _():
        out[...] = gather_rows(o_scr, slice(None)).astype(BF16)
        qkv_grad[...] = q_acc[...].astype(BF16)
        out_grad[...] = o_acc[...].T.astype(BF16)


def time_forward_kernel(owned, local, direct, recv, w, allowed, out, normed, grad, qkv, scr, o_scr):
    width = normed.shape[1]
    half = grad.shape[0]
    steps = owned * local
    groups = recv.shape[0] // steps
    length = groups * local
    if direct:
        for s in range(groups):
            block = recv[s * steps : (s + 1) * steps, :].astype(F32)
            scr[:, s * local : (s + 1) * local, :] = block.reshape(owned, local, width + half)
    may = allowed[...] > 0.0

    def one(e):
        at = pl.ds(pl.multiple_of(e * length, length), length)
        if direct:
            block = scr[e]
        else:
            block = recv[at, :].astype(F32)
        n = block[:, :width].astype(BF16)
        normed[at, :] = n
        grad[:, at] = block[:, width:].T.astype(BF16)
        mine = dot(w[...], n, 1, 1).astype(BF16)
        qkv[:, at] = mine
        outs = []
        for h in range(half // HEAD_DIM):
            q, k, v = head_rows(mine, h, half)
            rounded = attention_weights(q, k, may).astype(BF16)
            outs.append(dot(v, rounded).astype(BF16))
        o = jnp.concatenate(outs, axis=0).astype(F32).T
        if direct:
            o_scr[e] = o
        else:
            out[at, :] = o.astype(BF16)

    together = next(n for n in (5, 3, 2, 1) if owned % n == 0)

    @pl.loop(0, owned // together)
    def _(i):
        for e in range(together):
            one(i * together + e)

    if direct:
        for s in range(groups):
            block = o_scr[:, s * local : (s + 1) * local, :]
            out[s * steps : (s + 1) * steps, :] = block.reshape(steps, half).astype(BF16)


def time_backward_kernel(length, normed, grad, qkv, allowed, qkv_grad, acc):
    i = pl.program_id(0)
    half = grad.shape[0]
    may = allowed[...] > 0.0

    @pl.when(i == 0)
    def _():
        acc[...] = jnp.zeros_like(acc)

    both = []
    for e in range(normed.shape[0] // length):
        at = slice(e * length, (e + 1) * length)
        mine, g = qkv[:, at], grad[:, at]
        grads = [[], [], []]
        for h in range(half // HEAD_DIM):
            q, k, v = head_rows(mine, h, half)
            gh = g[h * HEAD_DIM : (h + 1) * HEAD_DIM, :]
            weights = attention_weights(q, k, may)
            found = attention_grads(q, k, v, gh, weights, weights.astype(BF16))
            for part, value in zip(grads, found):
                part.append(value)
        both.append(jnp.concatenate(grads[0] + grads[1] + grads[2], axis=0))
    acc[...] += dot(jnp.concatenate(both, axis=1), normed[...])

    @pl.when(i == pl.num_programs(0) - 1)
    def _():
        qkv_grad[...] = acc[...].astype(BF16)


def finish_kernel(tokens, mask, mask_token, space, time, w_out, cot, layer_out, out_grad, acc):
    i = pl.program_id(0)

    @pl.when(i == 0)
    def _():
        acc[...] = jnp.zeros_like(acc)

    t = time[...]
    attended = jnp.concatenate([space[...], t], axis=1)
    masked = masked_rows(tokens[...], mask[...], mask_token[...])
    layer_out[...] = (masked + dot(attended, w_out[...])).astype(BF16)
    acc[...] += dot(cot[...], t, 0, 0)

    @pl.when(i == pl.num_programs(0) - 1)
    def _():
        out_grad[...] = acc[...].astype(BF16)


def shape(rows, columns, kind=BF16):
    return jax.ShapeDtypeStruct((rows, columns), kind)


def sum_shares(terms):
    total = terms[0].astype(F32)
    for s in range(1, terms.shape[0]):
        total = total + terms[s].astype(F32)
    return total


def sum_pair(value):
    groups = lax.axis_size("seq")
    pairs = groups // 2
    value = value.reshape(pairs, 2, value.shape[0] // groups, value.shape[1])
    odd = lax.axis_index("seq") % 2 == 1
    sent = jnp.where(odd, value[:, 0], value[:, 1])
    kept = jnp.where(odd, value[:, 1], value[:, 0])
    got = lax.ppermute(sent, "seq", [(i, i ^ 1) for i in range(groups)])
    return (kept.astype(F32) + got.astype(F32)).astype(BF16)


def reduce_pairs(both, scale):
    groups = lax.axis_size("seq")
    sides = [list(range(side, groups, 2)) for side in range(2)]
    terms = lax.all_to_all(both, "seq", split_axis=0, concat_axis=0, axis_index_groups=sides)
    total = sum_shares(terms).astype(BF16)
    if lax.axis_size("dp") == 2:
        other = lax.ppermute(total, "dp", [(0, 1), (1, 0)])
        whole = total.astype(F32) + other.astype(F32)
    else:
        whole = sum_shares(lax.all_gather(total, "dp"))
    return total, whole * scale


def shards(tokens, patch_mask, mask_token, gain, w_qkv, w_out, block_ids, temporal_mask, cotangent):
    record_count, electrodes, local, width = tokens.shape
    half = width // 2
    groups = lax.axis_size("seq")
    owned = electrodes // groups
    length = groups * local
    count = electrodes * local
    tile = min(256, count)
    steps = count // tile
    tokens_flat = tokens.reshape(count, width)
    cot = cotangent.reshape(count, width)
    mask = patch_mask.reshape(count, 1).astype(F32)
    mask_token = mask_token.reshape(1, width)
    gain = gain.reshape(1, width)
    ids = block_ids.astype(F32)
    blocks = temporal_mask.shape[0]
    onehot = (
        jnp.arange(length)[:, None] // (length // blocks) == jnp.arange(blocks)[None, :]
    ).astype(F32)
    allowed = jnp.dot(jnp.dot(onehot, temporal_mask.astype(F32)), onehot.T).T
    w_rows = w_qkv.T

    step = max(1, 16 // local)
    owned_first = owned * 5 // 8 // step * step
    portions = (owned_first, owned - owned_first)
    share = tuple(portion * local for portion in portions)
    normed, grad_space, send_first, send_second = pl.pallas_call(
        functools.partial(prepare_kernel, share),
        grid=(steps,),
        in_specs=[
            rows_of(tile, width), rows_of(tile, 1), full((1, width)), full((1, width)),
            full((width, width)), rows_of(tile, width),
        ],
        out_specs=[
            rows_of(tile, width), rows_of(tile, half),
            rows_of(tile // (owned * local) * share[0], width + half),
            rows_of(tile // (owned * local) * share[1], width + half),
        ],
        out_shape=[
            shape(count, width), shape(count, half),
            shape(groups * share[0], width + half), shape(groups * share[1], width + half),
        ],
        compiler_params=params(),
        cost_estimate=pl.CostEstimate(
            flops=2 * count * width * width, bytes_accessed=9 * count * width, transcendentals=0
        ),
    )(tokens_flat, mask, mask_token, gain, w_out, cot)

    direct = local % 8 == 0

    def to_electrodes(send, portion):
        recv = lax.all_to_all(
            send.reshape(groups, portion, local, width + half), "seq",
            split_axis=0, concat_axis=0,
        )
        if not direct:
            recv = jnp.swapaxes(recv, 0, 1)
        return recv.reshape(portion * length, width + half)

    recv_first = to_electrodes(send_first, portions[0])

    space_out, grad_qkv_space, grad_out_space = pl.pallas_call(
        functools.partial(space_kernel, local),
        grid=(local,),
        in_specs=[
            full((count, width)), full((count, half)), full((count, width)),
            full((3 * half, width)), full((electrodes, 1)), full((1, electrodes)),
        ],
        out_specs=[full((count, half)), full((3 * half, width)), full((width, half))],
        out_shape=[shape(count, half), shape(3 * half, width), shape(width, half)],
        scratch_shapes=[
            pltpu.VMEM((width // LANES, count, LANES), F32),
            pltpu.VMEM((half // LANES, count, LANES), F32),
            pltpu.VMEM((width // LANES, count, LANES), F32),
            pltpu.VMEM((half // LANES, count, LANES), F32),
            pltpu.VMEM((3 * half, width), F32),
            pltpu.VMEM((half, width), F32),
        ],
        compiler_params=params(),
        cost_estimate=pl.CostEstimate(
            flops=32 * count * width * width, bytes_accessed=8 * count * width, transcendentals=0
        ),
    )(normed, grad_space, cot, w_rows, ids.reshape(electrodes, 1), ids.reshape(1, electrodes))

    recv_first, send_second, space_out = lax.optimization_barrier(
        (recv_first, send_second, space_out)
    )
    recv_second = to_electrodes(send_second, portions[1])

    def time_forward(recv, portion):
        some = portion * length
        return pl.pallas_call(
            functools.partial(time_forward_kernel, portion, local, direct),
            grid=(1,),
            in_specs=[
                full((some, width + half)),
                pl.BlockSpec((3 * half, width), lambda i: (1, 0)),
                full((length, length)),
            ],
            out_specs=[
                full((some, half)), full((some, width)), full((half, some)),
                full((3 * half, some)),
            ],
            out_shape=[
                shape(some, half), shape(some, width), shape(half, some), shape(3 * half, some),
            ],
            scratch_shapes=[
                pltpu.VMEM((portion, length, width + half), F32),
                pltpu.VMEM((portion, length, half), F32),
            ],
            compiler_params=params(),
            cost_estimate=pl.CostEstimate(
                flops=16 * some * width * width, bytes_accessed=8 * some * width,
                transcendentals=0,
            ),
        )(recv, w_rows, allowed)

    def time_backward(normed_time, grad_time, qkv_time):
        some = normed_time.shape[0]
        pair = 2 * length if some % (2 * length) == 0 else length
        return pl.pallas_call(
            functools.partial(time_backward_kernel, length),
            grid=(some // pair,),
            in_specs=[
                rows_of(pair, width), columns_of(half, pair), columns_of(3 * half, pair),
                full((length, length)),
            ],
            out_specs=full((3 * half, width)),
            out_shape=shape(3 * half, width),
            scratch_shapes=[pltpu.VMEM((3 * half, width), F32)],
            compiler_params=params(),
            cost_estimate=pl.CostEstimate(
                flops=24 * some * width * width, bytes_accessed=8 * some * width,
                transcendentals=0,
            ),
        )(normed_time, grad_time, qkv_time, allowed)

    time_first, *kept_first = time_forward(recv_first, portions[0])
    recv_second, time_first = lax.optimization_barrier((recv_second, time_first))
    time_second, *kept_second = time_forward(recv_second, portions[1])
    time_second, kept_first = lax.optimization_barrier((time_second, kept_first))
    grad_qkv_first = time_backward(*kept_first)

    def by_group(out, portion):
        if not direct:
            out = jnp.swapaxes(out.reshape(portion, groups, local, half), 0, 1)
        return out.reshape(groups, portion * local, half)

    back = jnp.concatenate(
        [by_group(time_first, portions[0]), by_group(time_second, portions[1])], axis=1
    )
    time_back = lax.all_to_all(back, "seq", split_axis=0, concat_axis=0).reshape(count, half)
    grad_qkv_second = time_backward(*kept_second)
    grad_qkv_time = (grad_qkv_first.astype(F32) + grad_qkv_second.astype(F32)).astype(BF16)
    grad_qkv = jnp.concatenate([grad_qkv_space, grad_qkv_time], axis=0)
    time_back, pair_qkv = lax.optimization_barrier((time_back, sum_pair(grad_qkv)))
    scale = 1.0 / math.sqrt(record_count * lax.axis_size("dp") * electrodes * length)
    total_qkv, share_qkv = reduce_pairs(pair_qkv, scale)

    layer_out, grad_out_time = pl.pallas_call(
        finish_kernel,
        grid=(steps,),
        in_specs=[
            rows_of(tile, width), rows_of(tile, 1), full((1, width)), rows_of(tile, half),
            rows_of(tile, half), full((width, width)), rows_of(tile, width),
        ],
        out_specs=[rows_of(tile, width), full((width, half))],
        out_shape=[shape(count, width), shape(width, half)],
        scratch_shapes=[pltpu.VMEM((width, half), F32)],
        compiler_params=params(),
        cost_estimate=pl.CostEstimate(
            flops=4 * count * width * width, bytes_accessed=8 * count * width, transcendentals=0
        ),
    )(tokens_flat, mask, mask_token, space_out, time_back, w_out, cot)

    grad_out = jnp.concatenate([grad_out_space, grad_out_time], axis=1)
    total_qkv, pair_out = lax.optimization_barrier((total_qkv, sum_pair(grad_out)))
    _, share_out = reduce_pairs(pair_out, scale)
    return layer_out.reshape(tokens.shape), share_qkv, share_out


def solution(mesh):
    return jax.shard_map(
        shards,
        mesh=mesh,
        in_specs=(
            P("dp", None, "seq", None),
            P("dp", None, "seq"),
            P(),
            P(),
            P(),
            P(),
            P(),
            P(),
            P("dp", None, "seq", None),
        ),
        out_specs=(P("dp", None, "seq", None), P("seq", None), P("seq", None)),
        check_vma=False,
    )
```

```python
import functools
import math

import jax
import jax.numpy as jnp
from jax import lax
from jax.experimental import pallas as pl
from jax.experimental.pallas import tpu as pltpu
from jax.sharding import PartitionSpec as P

HEADS = 8
HEAD_DIM = 64
NORM_EPS = 1e-05
LANES = 128
F32 = jnp.float32
BF16 = jnp.bfloat16
VMEM_BYTES = 48 * 1024 * 1024


def dot(a, b, ca=1, cb=0):
    return lax.dot_general(a, b, (((ca,), (cb,)), ((), ())), preferred_element_type=F32)


def params():
    return pltpu.CompilerParams(vmem_limit_bytes=VMEM_BYTES)


def full(shape):
    return pl.BlockSpec(shape, lambda i: (0,) * len(shape))


def rows_of(rows, columns):
    return pl.BlockSpec((rows, columns), lambda i: (i, 0))


def columns_of(rows, columns):
    return pl.BlockSpec((rows, columns), lambda i: (0, i))


def scatter_rows(scratch, value, rows=slice(None)):
    for c in range(scratch.shape[0]):
        scratch[c, rows, :] = value[:, c * LANES : (c + 1) * LANES].astype(F32)


def gather_rows(scratch, rows):
    return jnp.concatenate(
        [scratch[c, rows, :] for c in range(scratch.shape[0])], axis=1
    )


def masked_rows(tokens, mask, mask_token):
    return jnp.where(mask == 1.0, mask_token, tokens.astype(F32))


def attention_weights(q, k, allowed):
    exponent = jnp.where(allowed, jnp.exp(dot(k, q, 0, 0)), 0.0)
    return exponent * (1.0 / jnp.sum(exponent, axis=0, keepdims=True))


def attention_grads(q, k, v, g, weights, rounded):
    grad_v = dot(g, rounded, 1, 1).astype(BF16)
    grad_w = dot(v, g, 0, 0)
    inner = jnp.sum(grad_w * weights, axis=0, keepdims=True)
    grad_s = (weights * (grad_w - inner)).astype(BF16)
    grad_q = (dot(k, grad_s) * (HEAD_DIM**-0.5)).astype(BF16)
    grad_k = dot(q, grad_s, 1, 1).astype(BF16)
    return grad_q, grad_k, grad_v


def head_rows(qkv, h, half):
    at = h * HEAD_DIM
    q, k, v = [qkv[part * half + at : part * half + at + HEAD_DIM, :] for part in range(3)]
    return (q.astype(F32) * (HEAD_DIM**-0.5)).astype(BF16), k, v


def prepare_kernel(
    share, tokens, mask, mask_token, gain, w_out, cot, normed, grad_space, first, second
):
    width = tokens.shape[1]
    half = width // 2
    masked = masked_rows(tokens[...], mask[...], mask_token[...])
    centred = masked - jnp.mean(masked, axis=-1, keepdims=True)
    spread = jnp.mean(centred * centred, axis=-1, keepdims=True)
    n = (centred * lax.rsqrt(spread + NORM_EPS) * gain[...]).astype(BF16)
    normed[...] = n
    grad = dot(cot[...], w_out[...], 1, 1).astype(BF16)
    grad_space[...] = grad[:, :half]
    both = sum(share)
    for s in range(tokens.shape[0] // both):
        start = s * both
        for size, send in zip(share, (first, second)):
            to = slice(s * size, (s + 1) * size)
            at = slice(start, start + size)
            send[to, :width] = n[at, :]
            send[to, width:] = grad[at, half:]
            start += size


def space_kernel(
    patches, normed, grad, cot, w, id_col, id_row, out, qkv_grad, out_grad,
    n_scr, g_scr, c_scr, o_scr, q_acc, o_acc,
):
    p = pl.program_id(0)
    rows = normed.shape[0]
    half = grad.shape[1]
    electrodes = id_col.shape[0]

    @pl.when(p == 0)
    def _():
        scatter_rows(n_scr, normed[...])
        scatter_rows(g_scr, grad[...])
        scatter_rows(c_scr, cot[...])
        q_acc[...] = jnp.zeros_like(q_acc)
        o_acc[...] = jnp.zeros_like(o_acc)

    mine = pl.ds(p, electrodes, stride=patches)
    n = gather_rows(n_scr, mine).astype(BF16)
    g = gather_rows(g_scr, mine).T.astype(BF16)
    c = gather_rows(c_scr, mine).astype(BF16)
    allowed = id_col[...] == id_row[...]
    qkv = dot(w[...], n, 1, 1).astype(BF16)
    outs, grads = [], [[], [], []]
    for h in range(half // HEAD_DIM):
        q, k, v = head_rows(qkv, h, half)
        gh = g[h * HEAD_DIM : (h + 1) * HEAD_DIM, :]
        weights = attention_weights(q, k, allowed)
        rounded = weights.astype(BF16)
        outs.append(dot(v, rounded).astype(BF16))
        for part, value in zip(grads, attention_grads(q, k, v, gh, weights, rounded)):
            part.append(value)
    o = jnp.concatenate(outs, axis=0)
    scatter_rows(o_scr, o.astype(F32).T, mine)
    projected_grad = jnp.concatenate(grads[0] + grads[1] + grads[2], axis=0)
    q_acc[...] += dot(projected_grad, n)
    o_acc[...] += dot(o, c)

    @pl.when(p == patches - 1)
    def _():
        out[...] = gather_rows(o_scr, slice(None)).astype(BF16)
        qkv_grad[...] = q_acc[...].astype(BF16)
        out_grad[...] = o_acc[...].T.astype(BF16)


def time_forward_kernel(owned, local, direct, recv, w, allowed, out, normed, grad, qkv, scr, o_scr):
    width = normed.shape[1]
    half = grad.shape[0]
    steps = owned * local
    groups = recv.shape[0] // steps
    length = groups * local
    if direct:
        for s in range(groups):
            block = recv[s * steps : (s + 1) * steps, :].astype(F32)
            scr[:, s * local : (s + 1) * local, :] = block.reshape(owned, local, width + half)
    may = allowed[...] > 0.0

    def one(e):
        at = pl.ds(pl.multiple_of(e * length, length), length)
        if direct:
            block = scr[e]
        else:
            block = recv[at, :].astype(F32)
        n = block[:, :width].astype(BF16)
        normed[at, :] = n
        grad[:, at] = block[:, width:].T.astype(BF16)
        mine = dot(w[...], n, 1, 1).astype(BF16)
        qkv[:, at] = mine
        outs = []
        for h in range(half // HEAD_DIM):
            q, k, v = head_rows(mine, h, half)
            rounded = attention_weights(q, k, may).astype(BF16)
            outs.append(dot(v, rounded).astype(BF16))
        o = jnp.concatenate(outs, axis=0).astype(F32).T
        if direct:
            o_scr[e] = o
        else:
            out[at, :] = o.astype(BF16)

    together = next(n for n in (5, 3, 2, 1) if owned % n == 0)

    @pl.loop(0, owned // together)
    def _(i):
        for e in range(together):
            one(i * together + e)

    if direct:
        for s in range(groups):
            block = o_scr[:, s * local : (s + 1) * local, :]
            out[s * steps : (s + 1) * steps, :] = block.reshape(steps, half).astype(BF16)


def time_backward_kernel(length, normed, grad, qkv, allowed, qkv_grad, acc):
    i = pl.program_id(0)
    half = grad.shape[0]
    may = allowed[...] > 0.0

    @pl.when(i == 0)
    def _():
        acc[...] = jnp.zeros_like(acc)

    both = []
    for e in range(normed.shape[0] // length):
        at = slice(e * length, (e + 1) * length)
        mine, g = qkv[:, at], grad[:, at]
        grads = [[], [], []]
        for h in range(half // HEAD_DIM):
            q, k, v = head_rows(mine, h, half)
            gh = g[h * HEAD_DIM : (h + 1) * HEAD_DIM, :]
            weights = attention_weights(q, k, may)
            found = attention_grads(q, k, v, gh, weights, weights.astype(BF16))
            for part, value in zip(grads, found):
                part.append(value)
        both.append(jnp.concatenate(grads[0] + grads[1] + grads[2], axis=0))
    acc[...] += dot(jnp.concatenate(both, axis=1), normed[...])

    @pl.when(i == pl.num_programs(0) - 1)
    def _():
        qkv_grad[...] = acc[...].astype(BF16)


def finish_kernel(tokens, mask, mask_token, space, time, w_out, cot, layer_out, out_grad, acc):
    i = pl.program_id(0)

    @pl.when(i == 0)
    def _():
        acc[...] = jnp.zeros_like(acc)

    t = time[...]
    attended = jnp.concatenate([space[...], t], axis=1)
    masked = masked_rows(tokens[...], mask[...], mask_token[...])
    layer_out[...] = (masked + dot(attended, w_out[...])).astype(BF16)
    acc[...] += dot(cot[...], t, 0, 0)

    @pl.when(i == pl.num_programs(0) - 1)
    def _():
        out_grad[...] = acc[...].astype(BF16)


def shape(rows, columns, kind=BF16):
    return jax.ShapeDtypeStruct((rows, columns), kind)


def sum_shares(terms):
    total = terms[0].astype(F32)
    for s in range(1, terms.shape[0]):
        total = total + terms[s].astype(F32)
    return total


def sum_pair(value):
    groups = lax.axis_size("seq")
    pairs = groups // 2
    value = value.reshape(pairs, 2, value.shape[0] // groups, value.shape[1])
    odd = lax.axis_index("seq") % 2 == 1
    sent = jnp.where(odd, value[:, 0], value[:, 1])
    kept = jnp.where(odd, value[:, 1], value[:, 0])
    got = lax.ppermute(sent, "seq", [(i, i ^ 1) for i in range(groups)])
    return (kept.astype(F32) + got.astype(F32)).astype(BF16)


def reduce_pairs(both, scale):
    groups = lax.axis_size("seq")
    sides = [list(range(side, groups, 2)) for side in range(2)]
    terms = lax.all_to_all(both, "seq", split_axis=0, concat_axis=0, axis_index_groups=sides)
    total = sum_shares(terms).astype(BF16)
    if lax.axis_size("dp") == 2:
        other = lax.ppermute(total, "dp", [(0, 1), (1, 0)])
        whole = total.astype(F32) + other.astype(F32)
    else:
        whole = sum_shares(lax.all_gather(total, "dp"))
    return total, whole * scale


def shards(tokens, patch_mask, mask_token, gain, w_qkv, w_out, block_ids, temporal_mask, cotangent):
    record_count, electrodes, local, width = tokens.shape
    half = width // 2
    groups = lax.axis_size("seq")
    owned = electrodes // groups
    length = groups * local
    count = electrodes * local
    tile = min(256, count)
    steps = count // tile
    tokens_flat = tokens.reshape(count, width)
    cot = cotangent.reshape(count, width)
    mask = patch_mask.reshape(count, 1).astype(F32)
    mask_token = mask_token.reshape(1, width)
    gain = gain.reshape(1, width)
    ids = block_ids.astype(F32)
    blocks = temporal_mask.shape[0]
    onehot = (
        jnp.arange(length)[:, None] // (length // blocks) == jnp.arange(blocks)[None, :]
    ).astype(F32)
    allowed = jnp.dot(jnp.dot(onehot, temporal_mask.astype(F32)), onehot.T).T
    w_rows = w_qkv.T

    step = max(1, 16 // local)
    owned_first = owned * 3 // 4 // step * step
    portions = (owned_first, owned - owned_first)
    share = tuple(portion * local for portion in portions)
    normed, grad_space, send_first, send_second = pl.pallas_call(
        functools.partial(prepare_kernel, share),
        grid=(steps,),
        in_specs=[
            rows_of(tile, width), rows_of(tile, 1), full((1, width)), full((1, width)),
            full((width, width)), rows_of(tile, width),
        ],
        out_specs=[
            rows_of(tile, width), rows_of(tile, half),
            rows_of(tile // (owned * local) * share[0], width + half),
            rows_of(tile // (owned * local) * share[1], width + half),
        ],
        out_shape=[
            shape(count, width), shape(count, half),
            shape(groups * share[0], width + half), shape(groups * share[1], width + half),
        ],
        compiler_params=params(),
        cost_estimate=pl.CostEstimate(
            flops=2 * count * width * width, bytes_accessed=9 * count * width, transcendentals=0
        ),
    )(tokens_flat, mask, mask_token, gain, w_out, cot)

    direct = local % 8 == 0

    def to_electrodes(send, portion):
        recv = lax.all_to_all(
            send.reshape(groups, portion, local, width + half), "seq",
            split_axis=0, concat_axis=0,
        )
        if not direct:
            recv = jnp.swapaxes(recv, 0, 1)
        return recv.reshape(portion * length, width + half)

    recv_first = to_electrodes(send_first, portions[0])

    space_out, grad_qkv_space, grad_out_space = pl.pallas_call(
        functools.partial(space_kernel, local),
        grid=(local,),
        in_specs=[
            full((count, width)), full((count, half)), full((count, width)),
            full((3 * half, width)), full((electrodes, 1)), full((1, electrodes)),
        ],
        out_specs=[full((count, half)), full((3 * half, width)), full((width, half))],
        out_shape=[shape(count, half), shape(3 * half, width), shape(width, half)],
        scratch_shapes=[
            pltpu.VMEM((width // LANES, count, LANES), F32),
            pltpu.VMEM((half // LANES, count, LANES), F32),
            pltpu.VMEM((width // LANES, count, LANES), F32),
            pltpu.VMEM((half // LANES, count, LANES), F32),
            pltpu.VMEM((3 * half, width), F32),
            pltpu.VMEM((half, width), F32),
        ],
        compiler_params=params(),
        cost_estimate=pl.CostEstimate(
            flops=32 * count * width * width, bytes_accessed=8 * count * width, transcendentals=0
        ),
    )(normed, grad_space, cot, w_rows, ids.reshape(electrodes, 1), ids.reshape(1, electrodes))

    recv_first, send_second, space_out = lax.optimization_barrier(
        (recv_first, send_second, space_out)
    )
    recv_second = to_electrodes(send_second, portions[1])

    def time_forward(recv, portion):
        some = portion * length
        return pl.pallas_call(
            functools.partial(time_forward_kernel, portion, local, direct),
            grid=(1,),
            in_specs=[
                full((some, width + half)),
                pl.BlockSpec((3 * half, width), lambda i: (1, 0)),
                full((length, length)),
            ],
            out_specs=[
                full((some, half)), full((some, width)), full((half, some)),
                full((3 * half, some)),
            ],
            out_shape=[
                shape(some, half), shape(some, width), shape(half, some), shape(3 * half, some),
            ],
            scratch_shapes=[
                pltpu.VMEM((portion, length, width + half), F32),
                pltpu.VMEM((portion, length, half), F32),
            ],
            compiler_params=params(),
            cost_estimate=pl.CostEstimate(
                flops=16 * some * width * width, bytes_accessed=8 * some * width,
                transcendentals=0,
            ),
        )(recv, w_rows, allowed)

    def time_backward(normed_time, grad_time, qkv_time):
        some = normed_time.shape[0]
        pair = 2 * length if some % (2 * length) == 0 else length
        return pl.pallas_call(
            functools.partial(time_backward_kernel, length),
            grid=(some // pair,),
            in_specs=[
                rows_of(pair, width), columns_of(half, pair), columns_of(3 * half, pair),
                full((length, length)),
            ],
            out_specs=full((3 * half, width)),
            out_shape=shape(3 * half, width),
            scratch_shapes=[pltpu.VMEM((3 * half, width), F32)],
            compiler_params=params(),
            cost_estimate=pl.CostEstimate(
                flops=24 * some * width * width, bytes_accessed=8 * some * width,
                transcendentals=0,
            ),
        )(normed_time, grad_time, qkv_time, allowed)

    time_first, *kept_first = time_forward(recv_first, portions[0])
    recv_second, time_first = lax.optimization_barrier((recv_second, time_first))
    time_second, *kept_second = time_forward(recv_second, portions[1])
    time_second, kept_first = lax.optimization_barrier((time_second, kept_first))
    grad_qkv_first = time_backward(*kept_first)

    def by_group(out, portion):
        if not direct:
            out = jnp.swapaxes(out.reshape(portion, groups, local, half), 0, 1)
        return out.reshape(groups, portion * local, half)

    back = jnp.concatenate(
        [by_group(time_first, portions[0]), by_group(time_second, portions[1])], axis=1
    )
    time_back = lax.all_to_all(back, "seq", split_axis=0, concat_axis=0).reshape(count, half)
    grad_qkv_second = time_backward(*kept_second)
    grad_qkv_time = (grad_qkv_first.astype(F32) + grad_qkv_second.astype(F32)).astype(BF16)
    grad_qkv = jnp.concatenate([grad_qkv_space, grad_qkv_time], axis=0)
    time_back, pair_qkv = lax.optimization_barrier((time_back, sum_pair(grad_qkv)))
    scale = 1.0 / math.sqrt(record_count * lax.axis_size("dp") * electrodes * length)
    total_qkv, share_qkv = reduce_pairs(pair_qkv, scale)

    layer_out, grad_out_time = pl.pallas_call(
        finish_kernel,
        grid=(steps,),
        in_specs=[
            rows_of(tile, width), rows_of(tile, 1), full((1, width)), rows_of(tile, half),
            rows_of(tile, half), full((width, width)), rows_of(tile, width),
        ],
        out_specs=[rows_of(tile, width), full((width, half))],
        out_shape=[shape(count, width), shape(width, half)],
        scratch_shapes=[pltpu.VMEM((width, half), F32)],
        compiler_params=params(),
        cost_estimate=pl.CostEstimate(
            flops=4 * count * width * width, bytes_accessed=8 * count * width, transcendentals=0
        ),
    )(tokens_flat, mask, mask_token, space_out, time_back, w_out, cot)

    grad_out = jnp.concatenate([grad_out_space, grad_out_time], axis=1)
    total_qkv, pair_out = lax.optimization_barrier((total_qkv, sum_pair(grad_out)))
    _, share_out = reduce_pairs(pair_out, scale)
    return layer_out.reshape(tokens.shape), share_qkv, share_out


def solution(mesh):
    return jax.shard_map(
        shards,
        mesh=mesh,
        in_specs=(
            P("dp", None, "seq", None),
            P("dp", None, "seq"),
            P(),
            P(),
            P(),
            P(),
            P(),
            P(),
            P("dp", None, "seq", None),
        ),
        out_specs=(P("dp", None, "seq", None), P("seq", None), P("seq", None)),
        check_vma=False,
    )
```
